32 devices in a mesh: gx: 4 (over y, core), gy: 4 (over z), gz: 2 (over x).
Axes of the slice: x: 2, y: 2, z: 4, core: 2. Of those that a mesh axis runs over, the one named last changes fastest.
Arguments:
- positions: float32 [3, 4, 4, 2, 512], P(None, 'gx', 'gy', 'gz'), may hold values from -6 to 6
- velocity: float32 [3, 4, 4, 2, 512], P(None, 'gx', 'gy', 'gz'), may hold values from -7.2 to 7.2
- atom_eps: float32 [4, 4, 2, 512], P('gx', 'gy', 'gz'), may hold values from 0.5 to 2
- neighbours: int32 [4, 4, 2, 32, 512], P('gx', 'gy', 'gz'), may hold values from 0 to 511
- pair_live: int32 [4, 4, 2, 32, 512], P('gx', 'gy', 'gz'), may hold values 0 or 1
- event_count: int32 [4, 4, 2], P('gx', 'gy', 'gz'), may hold values from 0 to 16, as said below
- event_atoms: int32 [4, 4, 2, 16, 128], P('gx', 'gy', 'gz'), may hold values from 0 to 1023
- event_weight: float32 [4, 4, 2, 16], P('gx', 'gy', 'gz'), may hold values from 0.2 to 1
- template_map: float32 [128, 128], replicated, may hold values from -0.5 to 0.5
Outputs:
- final_positions: float32 [3, 4, 4, 2, 512], P(None, 'gx', 'gy', 'gz')
- final_velocity: float32 [3, 4, 4, 2, 512], P(None, 'gx', 'gy', 'gz')
The draws below stay inside these ranges and needn't reach their ends.
Inputs may be any that keep to these rules, and one draw needn't show every extreme that they name: `event_count`: in every column of domains along the third dimension, the counts add up to at most 32, and one domain of the column holds 16.
All inputs are finite; a program needn't handle non-finite values. No bound on the sum of `pair_live` on one device may be relied on, other than what follows from the above.
Results may differ from the reference program's by a relative error of at most 0.0003.
Values sent between devices are 32-bit elements; how exact they have to be, the bound alone decides.
A program may use at most 64 MiB of HBM per device.

```python
import math
import jax
import jax.numpy as jnp
from jax import lax

ATOMS_DEV = 512
EV_DEV = 16
NEIGH = 32
TEMPLATE = 128
FIRE_STEPS = 2
DOM_X = 4
DOM_Y = 4
DOM_Z = 2


def draw_velocity(key, part):
    shape = (3, DOM_X, DOM_Y, DOM_Z, ATOMS_DEV)
    base = jax.random.truncated_normal(key, -4.0, 4.0, shape, jnp.float32)
    domains = DOM_X * DOM_Y * DOM_Z
    ordering = jnp.arange(domains, dtype=jnp.float32).reshape(1, DOM_X, DOM_Y, DOM_Z, 1) / max(domains - 1, 1)
    scales = 0.6 * 3.0 ** ordering
    return (base * scales).astype(jnp.float32)


def fill_column(column_key):
    first_key = jax.random.fold_in(column_key, 1)
    second_key = jax.random.fold_in(column_key, 2)
    full_slot = jax.random.randint(first_key, (), 0, DOM_Z)
    cuts = jnp.sort(jax.random.randint(second_key, (DOM_Z - 1,), 0, EV_DEV + 1))
    edges = jnp.concatenate([jnp.zeros((1,), jnp.int32), cuts.astype(jnp.int32)])
    others = edges[1:] - edges[:-1]
    places = jnp.arange(DOM_Z, dtype=jnp.int32)
    lookup = jnp.clip(jnp.where(places > full_slot, places - 1, places), 0, DOM_Z - 2)
    return jnp.where(places == full_slot, EV_DEV, others[lookup]).astype(jnp.int32)


def draw_event_count(key, part):
    column_keys = jax.random.split(jax.random.fold_in(key, 3), DOM_X * DOM_Y)
    return jax.vmap(fill_column)(column_keys).reshape(DOM_X, DOM_Y, DOM_Z)


def set_ends(values, key, smallest, high):
    place = [jax.random.randint(jax.random.fold_in(key, axis), (), 0, length) for axis, length in enumerate(values.shape)]
    longest = values.shape.index(max(values.shape))
    neighbour = place[:longest] + [(place[longest] + 1) % values.shape[longest]] + place[longest + 1:]
    return values.at[tuple(place)].set(smallest).at[tuple(neighbour)].set(high)


def shard_levels(own_key, extent, cuts, smallest, largest):
    gain, own = 1.0, jax.random.fold_in(own_key, 6)
    for dim, blocks in cuts:
        draws = jnp.exp(jax.random.uniform(jax.random.fold_in(own, dim), (blocks,), jnp.float32, smallest / len(cuts), largest / len(cuts)))
        gain = gain * jnp.repeat(draws, extent[dim] // blocks).reshape([-1 if axis == dim else 1 for axis in range(len(extent))])
    return gain


def normal_values(key, shape, deviation, bound, shards=(), kind=jnp.bfloat16):
    drawn = deviation * jax.random.normal(key, shape, jnp.float32)
    if shards:
        drawn = drawn * shard_levels(key, shape, shards, -0.22, 0.18)
    return jnp.clip(drawn, -bound, bound).astype(kind)


def setup_inputs(seed: int = 0) -> dict:
    splits = jax.random.split(jax.random.key(seed), 10)
    return {
        "positions": normal_values(splits[0], (3, DOM_X, DOM_Y, DOM_Z, ATOMS_DEV), 1.0, 6.0, ((1, 4), (2, 4), (3, 2)), jnp.float32),
        "velocity": draw_velocity(jax.random.fold_in(splits[9], 71), 0),
        "atom_eps": jnp.clip(jnp.exp(math.log(2.0) - 1.3862944 * jax.random.uniform(splits[2], (DOM_X, DOM_Y, DOM_Z, ATOMS_DEV), jnp.float32) ** shard_levels(splits[2], (DOM_X, DOM_Y, DOM_Z, ATOMS_DEV), ((0, 4), (1, 4), (2, 2)), -0.2, 0.2)), 0.5, 2.0),
        "neighbours": set_ends(jax.random.randint(splits[3], (DOM_X, DOM_Y, DOM_Z, NEIGH, ATOMS_DEV), 0, ATOMS_DEV), jax.random.fold_in(splits[3], 1), 0, ATOMS_DEV - 1).astype(jnp.int32),
        "pair_live": set_ends((jax.random.randint(splits[4], (DOM_X, DOM_Y, DOM_Z, NEIGH, ATOMS_DEV), 0, 4) < 3).astype(jnp.int32), jax.random.fold_in(splits[4], 1), 0, 1),
        "event_count": draw_event_count(jax.random.fold_in(splits[9], 71), 0),
        "event_atoms": set_ends(jax.random.randint(splits[6], (DOM_X, DOM_Y, DOM_Z, EV_DEV, TEMPLATE), 0, DOM_Z * ATOMS_DEV), jax.random.fold_in(splits[6], 1), 0, (DOM_Z * ATOMS_DEV) - 1).astype(jnp.int32),
        "event_weight": jnp.clip(jnp.exp(math.log(1.0) - 1.609438 * jax.random.uniform(splits[7], (DOM_X, DOM_Y, DOM_Z, EV_DEV), jnp.float32) ** shard_levels(splits[7], (DOM_X, DOM_Y, DOM_Z, EV_DEV), ((0, 4), (1, 4), (2, 2)), -0.2, 0.2)), 0.2, 1.0),
        "template_map": normal_values(splits[8], (TEMPLATE, TEMPLATE), TEMPLATE ** -0.5, 0.5, (), jnp.float32),
    }


width_scale = 1.5
time_step = 0.1
mixing = 0.1
epsilon = 1e-06

def relax_events(group_positions, members, weights, template_map):
    gathered = jnp.take(group_positions, members, axis=1)
    centred = gathered - lax.optimization_barrier(jnp.mean(gathered, axis=2, keepdims=True))
    shifted = jnp.einsum('cnt,ts->cns', centred, template_map, precision=lax.Precision.HIGHEST)
    shifted = shifted * weights[None, :, None]
    flattened = members.reshape(-1)
    return jnp.zeros_like(group_positions).at[:, flattened].add(shifted.reshape(3, -1))

def pair_forces(neighbourhood, own_atoms, neighbour_rows, live_pairs):
    partner = jnp.take(neighbourhood, neighbour_rows, axis=1)
    separation = own_atoms[:3, None, :] - partner[:3]
    distance_sq = lax.optimization_barrier(jnp.sum(separation * separation, axis=0))
    strength = jnp.sqrt(own_atoms[3][None, :] * partner[3]) * live_pairs.astype(jnp.float32)
    strength = strength * jnp.exp(-distance_sq * (0.5 / (width_scale * width_scale))) / (width_scale * width_scale)
    return lax.optimization_barrier(jnp.sum(strength[None] * separation, axis=1))

def halo_blocks(packed, slab_index):
    pieces = []
    for offset_x in range(3):
        slab = lax.dynamic_index_in_dim(packed, (slab_index + offset_x - 1) % DOM_X, 1, False)
        for offset_y in range(3):
            for offset_z in range(3):
                pieces.append(jnp.roll(slab, (1 - offset_y, 1 - offset_z), axis=(1, 2)))
    stacked = jnp.stack(pieces, 1)
    return jnp.moveaxis(stacked, 1, 3).reshape(4, DOM_Y, DOM_Z, 27 * ATOMS_DEV)

def all_forces(moved_positions, atom_eps, neighbours, pair_live):
    packed = jnp.concatenate([moved_positions, atom_eps[None]], 0)
    offsets = (jnp.arange(NEIGH, dtype=jnp.int32) % 27 * ATOMS_DEV).astype(jnp.int32)
    rows_all = (neighbours + offsets[None, None, None, :, None]).astype(jnp.int32)

    def slab_forces(slab_index):
        neighbourhood = halo_blocks(packed, slab_index)
        own_atoms = lax.dynamic_index_in_dim(packed, slab_index, 1, False)
        neighbour_rows = lax.dynamic_index_in_dim(rows_all, slab_index, 0, False)
        live_pairs = lax.dynamic_index_in_dim(pair_live, slab_index, 0, False)
        inner = jax.vmap(pair_forces, (1, 1, 0, 0), 1)
        return jax.vmap(inner, (1, 1, 0, 0), 1)(neighbourhood, own_atoms, neighbour_rows, live_pairs)
    result = lax.map(slab_forces, jnp.arange(DOM_X, dtype=jnp.int32))
    return jnp.moveaxis(result, 0, 1)

def reference(positions, velocity, atom_eps, neighbours, pair_live, event_count, event_atoms, event_weight, template_map):
    columns = DOM_X * DOM_Y
    group_positions = jnp.moveaxis(positions.reshape(3, columns, DOM_Z * ATOMS_DEV), 1, 0)
    alive_mask = jnp.arange(EV_DEV, dtype=jnp.int32)[None, None, None, :] < event_count[..., None]
    weights = (event_weight * alive_mask.astype(event_weight.dtype)).reshape(columns, DOM_Z * EV_DEV)
    members = event_atoms.reshape(columns, DOM_Z * EV_DEV, TEMPLATE)
    displaced = jax.vmap(lambda grouped, chosen, scaled: relax_events(grouped, chosen, scaled, template_map))(group_positions, members, weights)
    moved_positions = positions + jnp.moveaxis(displaced, 0, 1).reshape(positions.shape)
    speeds = velocity
    for iteration in range(FIRE_STEPS):
        forces = all_forces(moved_positions, atom_eps, neighbours, pair_live)
        power_sum = jnp.sum(forces * speeds)
        speed_sq = jnp.sum(speeds * speeds)
        force_sq = jnp.sum(forces * forces)
        cosine = power_sum / (jnp.sqrt(speed_sq + epsilon) * jnp.sqrt(force_sq + epsilon))
        speed_ratio = jnp.sqrt((speed_sq + epsilon) / (force_sq + epsilon))
        speeds = 0.5 * (1.0 + cosine) * ((1.0 - mixing) * speeds + mixing * speed_ratio * forces)
        speeds = speeds + time_step * forces
        moved_positions = moved_positions + time_step * speeds
    return (moved_positions, speeds)
```

```python
import functools

import jax
import jax.numpy as jnp
from jax import lax
from jax.experimental import pallas as pl
from jax.experimental.pallas import tpu as pltpu
from jax.sharding import PartitionSpec as P

width_scale = 1.5
time_step = 0.1
mixing = 0.1
epsilon = 1e-06

MESH = pl.DeviceIdType.MESH
LANES = 128
ROWS = 16
DIRECT = 64


def lane_gather(table, index):
    return jnp.take_along_axis(table, index, axis=1, mode="promise_in_bounds")


def cycle_kernel(
    mesh_shape,
    pos_in,
    vel_in,
    eps_in,
    nbr_in,
    live_in,
    count_in,
    atoms_in,
    weight_in,
    map_in,
    pos_out,
    vel_out,
    pos_v,
    vel_v,
    eps_v,
    nbr,
    live,
    count_v,
    atoms,
    weight_v,
    tmap,
    col,
    moved,
    shifts,
    table,
    table2,
    speeds,
    forces,
    forces2,
    sums,
    local_sem,
    col_sem,
    send_sem,
    recv_sem,
    sum_send,
    sum_recv,
):
    nx, ny, nz = mesh_shape
    devices = nx * ny * nz
    x, y, z = lax.axis_index("gx"), lax.axis_index("gy"), lax.axis_index("gz")
    slots, atom_count = nbr.shape
    events, template = atoms.shape[1:]
    chunks = atom_count // LANES
    home = 13
    depth_offsets = (0, 1) if nz == 2 else (0, 1, 2)
    depths = len(depth_offsets)

    def peer(dx, dy, dz):
        return (
            lax.rem(x + dx + nx, nx),
            lax.rem(y + dy + ny, ny),
            lax.rem(z + dz + nz, nz),
        )

    def copies(j):
        dirs = [j] if nz > 2 or j % 3 != 0 else [j, j + 2]
        return [s for d in dirs for s in range(d, slots, 27)]

    around = [
        (a, b, c)
        for a in range(3)
        for b in range(3)
        for c in depth_offsets
        if (a, b, c) != (1, 1, 1)
    ]
    beside = [(a, b) for a in range(3) for b in range(3) if (a, b) != (1, 1)]
    if devices <= DIRECT:
        stages = [
            [
                (dx, dy, dz)
                for dx in range(nx)
                for dy in range(ny)
                for dz in range(nz)
                if (dx, dy, dz) != (0, 0, 0)
            ]
        ]
    else:
        stages = [
            [(d, 0, 0) for d in range(1, nx)],
            [(0, d, 0) for d in range(1, ny)],
            [(0, 0, d) for d in range(1, nz)],
        ]
    greeted = {((1 - a) % nx, (1 - b) % ny, (1 - c) % nz) for a, b, c in around}
    greeted |= {((a - 1) % nx, (b - 1) % ny, (c - 1) % nz) for a, b, c in around}
    greeted |= {offset for stage in stages for offset in stage}
    greeted |= {(0, 0, d) for d in range(1, nz)}
    greeted = sorted(greeted)

    own_atoms = atoms.at[z]
    pairs = [
        (pos_in, pos_v),
        (vel_in, vel_v),
        (eps_in, eps_v),
        (count_in, count_v),
        (weight_in, weight_v),
        (atoms_in, own_atoms),
        (map_in, tmap),
        (nbr_in, nbr),
        (live_in, live),
    ]
    loads = [
        pltpu.make_async_copy(src, dst, local_sem.at[i]) for i, (src, dst) in enumerate(pairs)
    ]
    for load in loads:
        load.start()
    barrier = pltpu.get_barrier_semaphore()
    for offset in greeted:
        pl.semaphore_signal(barrier, inc=1, device_id=peer(*offset), device_id_type=MESH)
    for load in loads[:6]:
        load.wait()

    for chunk in range(chunks):
        lanes = pl.ds(chunk * LANES, LANES)
        for i in range(3):
            row = i * chunks + chunk
            col[z, pl.ds(row, 1), :] = pos_v[i, :, lanes]
            speeds[pl.ds(home * ROWS + row, 1), :] = vel_v[i, :, lanes]
        row = 3 * chunks + chunk
        col[z, pl.ds(row, 1), :] = jnp.sqrt(eps_v[:, lanes])
        speeds[pl.ds(home * ROWS + row, 1), :] = jnp.zeros((1, LANES), jnp.float32)
    alive = lax.broadcasted_iota(jnp.int32, (1, events), 1) < count_v[...]
    live_weight = jnp.where(alive, weight_v[...], 0.0)
    spread = jnp.broadcast_to(live_weight, (events, events))
    diagonal = lax.broadcasted_iota(jnp.int32, (events, events), 0) == lax.broadcasted_iota(
        jnp.int32, (events, events), 1
    )
    column_weight = jnp.sum(jnp.where(diagonal, spread, 0.0), axis=1, keepdims=True)
    col[z, pl.ds(ROWS, events), :] = jnp.broadcast_to(column_weight, (events, LANES))

    pl.semaphore_wait(barrier, len(greeted))

    column_copies = []
    for d in range(1, nz):
        for part, ref in enumerate((col, atoms)):
            copy = pltpu.make_async_remote_copy(
                src_ref=ref.at[z],
                dst_ref=ref.at[z],
                send_sem=col_sem.at[0, part, d - 1],
                recv_sem=col_sem.at[1, part, d - 1],
                device_id=peer(0, 0, d),
                device_id_type=MESH,
            )
            copy.start()
            column_copies.append(copy)

    def send_around(ref, which):
        for a, b, c in around:
            j = (a * 3 + b) * 3 + c
            pltpu.make_async_remote_copy(
                src_ref=ref.at[pl.ds(home * ROWS, ROWS)],
                dst_ref=ref.at[pl.ds(j * ROWS, ROWS)],
                send_sem=send_sem.at[which],
                recv_sem=recv_sem.at[which],
                device_id=peer(1 - a, 1 - b, 1 - c),
                device_id_type=MESH,
            ).start()

    def wait_total(ref, rows, sem):
        part = ref.at[pl.ds(0, rows)]
        pltpu.make_async_copy(part, part, sem).wait()

    send_around(speeds, 0)
    for load in loads[6:]:
        load.wait()
    for copy in column_copies:
        copy.wait_recv()

    total_events = nz * events
    members = atoms[...].reshape(total_events, template)
    member_chunk = lax.shift_right_logical(members, 7)
    member_lane = members & (LANES - 1)
    weights = jnp.concatenate([col[d, pl.ds(ROWS, events), :] for d in range(nz)], axis=0)
    centred = []
    for i in range(3):
        taken = jnp.zeros((total_events, template), jnp.float32)
        for d in range(nz):
            for chunk in range(chunks):
                source = jnp.broadcast_to(
                    col[d, pl.ds(i * chunks + chunk, 1), :], (total_events, LANES)
                )
                picked = lane_gather(source, member_lane)
                taken = jnp.where(member_chunk == d * chunks + chunk, picked, taken)
        mean = jnp.sum(taken, axis=1, keepdims=True) * (1.0 / template)
        centred.append(taken - mean)
    shifted = jnp.dot(
        jnp.concatenate(centred, axis=0),
        tmap[...],
        precision=lax.Precision.HIGHEST,
        preferred_element_type=jnp.float32,
    )
    for i in range(3):
        shift = shifted[i * total_events : (i + 1) * total_events] * weights
        coarse = shift.astype(jnp.bfloat16).astype(jnp.float32)
        shifts[i] = coarse
        shifts[3 + i] = shift - coarse

    column_chunks = nz * chunks
    lane_row = lax.broadcasted_iota(jnp.int32, (LANES, template), 0)
    chunk_row = lax.broadcasted_iota(jnp.int32, (column_chunks, template), 0)
    summed = jnp.zeros((6 * column_chunks, LANES), jnp.float32)
    for first in range(0, total_events, 2):
        left, right = [], []
        for e in range(first, first + 2):
            here = member_chunk[e : e + 1] == chunk_row
            left.append(
                jnp.concatenate(
                    [
                        jnp.where(here, shifts[q, pl.ds(e, 1), :], 0.0)
                        for q in range(6)
                    ],
                    axis=0,
                )
            )
            right.append(jnp.where(member_lane[e : e + 1] == lane_row, 1.0, 0.0))
        summed = summed + lax.dot_general(
            jnp.concatenate(left, axis=1).astype(jnp.bfloat16),
            jnp.concatenate(right, axis=1).astype(jnp.bfloat16),
            (((1,), (1,)), ((), ())),
            preferred_element_type=jnp.float32,
        )
    half = 3 * column_chunks
    displaced = summed[:half] + summed[half:]
    for d in range(nz):
        pieces = [
            displaced[i * column_chunks + d * chunks : i * column_chunks + (d + 1) * chunks]
            for i in range(3)
        ]
        pieces.append(jnp.zeros((chunks, LANES), jnp.float32))
        moved[d] = col[d, pl.ds(0, ROWS), :] + jnp.concatenate(pieces, axis=0)

    for c in range(3):
        table[pl.ds((home - 1 + c) * ROWS, ROWS), :] = moved[lax.rem(z + c - 1 + nz, nz)]
    for a, b in beside:
        pltpu.make_async_remote_copy(
            src_ref=table.at[pl.ds((home - 1) * ROWS, depths * ROWS)],
            dst_ref=table.at[pl.ds((a * 3 + b) * 3 * ROWS, depths * ROWS)],
            send_sem=send_sem.at[1],
            recv_sem=recv_sem.at[1],
            device_id=peer(1 - a, 1 - b, 0),
            device_id_type=MESH,
        ).start()
    wait_total(table, len(beside) * depths * ROWS, recv_sem.at[1])
    for a, b in beside:
        for c in depth_offsets:
            j = (a * 3 + b) * 3 + c
            block = table[pl.ds(j * ROWS, ROWS), :]
            for s in copies(j)[1:]:
                table[pl.ds(s * ROWS, ROWS), :] = block
    for c in range(3):
        j = home - 1 + c
        for s in range(j + 27, slots, 27):
            table[pl.ds(s * ROWS, ROWS), :] = table[pl.ds(j * ROWS, ROWS), :]

    def pair_forces(where, result):
        total = [[jnp.zeros((8, LANES), jnp.float32)] * 3 for _ in range(chunks)]
        for group in range(slots // 8):
            source = [
                [
                    where[pl.ds(group * 8 * ROWS + i * chunks + t, 8, stride=ROWS), :]
                    for t in range(chunks)
                ]
                for i in range(4)
            ]
            for chunk in range(chunks):
                rows, lanes = pl.ds(group * 8, 8), pl.ds(chunk * LANES, LANES)
                index = nbr[rows, lanes]
                lane, part = index & (LANES - 1), lax.shift_right_logical(index, 7)
                partner = []
                for i in range(4):
                    picked = lane_gather(source[i][0], lane)
                    for t in range(1, chunks):
                        picked = jnp.where(part == t, lane_gather(source[i][t], lane), picked)
                    partner.append(picked)
                own = [
                    where[pl.ds(home * ROWS + i * chunks + chunk, 1), :] for i in range(4)
                ]
                apart = [own[i] - partner[i] for i in range(3)]
                square = apart[0] * apart[0] + apart[1] * apart[1] + apart[2] * apart[2]
                strength = (
                    own[3]
                    * partner[3]
                    * live[rows, lanes].astype(jnp.float32)
                    * jnp.exp(square * (-0.5 / (width_scale * width_scale)))
                    * (1.0 / (width_scale * width_scale))
                )
                total[chunk] = [total[chunk][i] + strength * apart[i] for i in range(3)]
        for chunk in range(chunks):
            for i in range(3):
                result[pl.ds(home * ROWS + i * chunks + chunk, 1), :] = jnp.sum(
                    total[chunk][i], axis=0, keepdims=True
                )
        result[pl.ds(home * ROWS + 3 * chunks, chunks), :] = jnp.zeros(
            (chunks, LANES), jnp.float32
        )

    def whole(value):
        return jnp.sum(jnp.sum(value, axis=0, keepdims=True), axis=1, keepdims=True)

    lane_index = lax.broadcasted_iota(jnp.int32, (1, LANES), 1)
    most = max(len(stage) for stage in stages) + 1

    def sum_start(force, speed, which):
        row = jnp.where(lane_index == 0, whole(force * speed), 0.0)
        row = jnp.where(lane_index == 1, whole(speed * speed), row)
        row = jnp.where(lane_index == 2, whole(force * force), row)
        return stage_start(row, which, 0)

    def stage_start(row, which, s):
        base = (which * len(stages) + s) * most
        sums[base] = row
        for slot, offset in enumerate(stages[s]):
            pltpu.make_async_remote_copy(
                src_ref=sums.at[base],
                dst_ref=sums.at[base + 1 + slot],
                send_sem=sum_send.at[which, s],
                recv_sem=sum_recv.at[which, s],
                device_id=peer(*offset),
                device_id_type=MESH,
            ).start()

    def sum_finish(which):
        for s, stage in enumerate(stages):
            base = (which * len(stages) + s) * most
            wait_total(sums, len(stage), sum_recv.at[which, s])
            row = jnp.sum(sums[pl.ds(base, len(stage) + 1)], axis=0)
            if s + 1 < len(stages):
                stage_start(row, which, s + 1)
        power, speed_sq, force_sq = row[:, 0:1], row[:, 1:2], row[:, 2:3]
        cosine = power / (jnp.sqrt(speed_sq + epsilon) * jnp.sqrt(force_sq + epsilon))
        ratio = jnp.sqrt((speed_sq + epsilon) / (force_sq + epsilon))
        keep = 0.5 * (1.0 + cosine)
        return keep * (1.0 - mixing), keep * mixing * ratio + time_step

    def block(ref, j):
        return ref[pl.ds(j * ROWS, ROWS), :]

    pair_forces(table, forces)
    send_around(forces, 2)
    sum_start(block(forces, home), block(speeds, home), 0)
    wait_total(speeds, len(around) * ROWS, recv_sem.at[0])
    old, new = sum_finish(0)
    wait_total(forces, len(around) * ROWS, recv_sem.at[2])
    for a, b, c in around + [(1, 1, 1)]:
        j = (a * 3 + b) * 3 + c
        later = block(table, j) + time_step * (
            old * block(speeds, j) + new * block(forces, j)
        )
        for s in copies(j):
            table2[pl.ds(s * ROWS, ROWS), :] = later
    speed = old * block(speeds, home) + new * block(forces, home)

    pair_forces(table2, forces2)
    force = block(forces2, home)
    sum_start(force, speed, 1)
    old, new = sum_finish(1)
    speed = old * speed + new * force
    place = block(table2, home) + time_step * speed
    for chunk in range(chunks):
        lanes = pl.ds(chunk * LANES, LANES)
        for i in range(3):
            row = i * chunks + chunk
            pos_out[i, :, lanes] = place[row : row + 1]
            vel_out[i, :, lanes] = speed[row : row + 1]

    for copy in column_copies:
        copy.wait_send()
    wait_total(speeds, len(around) * ROWS, send_sem.at[0])
    wait_total(table, len(beside) * depths * ROWS, send_sem.at[1])
    wait_total(forces, len(around) * ROWS, send_sem.at[2])
    for which in range(2):
        for s, stage in enumerate(stages):
            wait_total(sums, len(stage), sum_send.at[which, s])


def shards(
    mesh_shape,
    positions,
    velocity,
    atom_eps,
    neighbours,
    pair_live,
    event_count,
    event_atoms,
    event_weight,
    template_map,
):
    atom_count = positions.shape[4]
    slots = neighbours.shape[3]
    events, template = event_atoms.shape[3:]
    nx, ny, nz = mesh_shape
    devices = nx * ny * nz
    stages, most = (1, devices) if devices <= DIRECT else (3, max(mesh_shape))
    f32, i32 = jnp.float32, jnp.int32
    blocks = pltpu.VMEM((slots * ROWS, LANES), f32)
    outs = pl.pallas_call(
        functools.partial(cycle_kernel, mesh_shape),
        out_shape=[jax.ShapeDtypeStruct((3, 1, atom_count), f32)] * 2,
        in_specs=[pl.BlockSpec(memory_space=pl.ANY)] * 9,
        out_specs=[pl.BlockSpec(memory_space=pltpu.VMEM)] * 2,
        scratch_shapes=[
            pltpu.VMEM((3, 1, atom_count), f32),
            pltpu.VMEM((3, 1, atom_count), f32),
            pltpu.VMEM((1, atom_count), f32),
            pltpu.VMEM((slots, atom_count), i32),
            pltpu.VMEM((slots, atom_count), i32),
            pltpu.VMEM((1, 1), i32),
            pltpu.VMEM((nz, events, template), i32),
            pltpu.VMEM((1, events), f32),
            pltpu.VMEM((template, template), f32),
            pltpu.VMEM((nz, ROWS + events, LANES), f32),
            pltpu.VMEM((nz, ROWS, LANES), f32),
            pltpu.VMEM((6, nz * events, template), f32),
            blocks,
            blocks,
            blocks,
            blocks,
            blocks,
            pltpu.VMEM((2 * stages * most, 1, LANES), f32),
            pltpu.SemaphoreType.DMA((9,)),
            pltpu.SemaphoreType.DMA((2, 2, nz - 1)),
            pltpu.SemaphoreType.DMA((3,)),
            pltpu.SemaphoreType.DMA((3,)),
            pltpu.SemaphoreType.DMA((2, stages)),
            pltpu.SemaphoreType.DMA((2, stages)),
        ],
        compiler_params=pltpu.CompilerParams(
            collective_id=0, has_side_effects=True, vmem_limit_bytes=32 * 1024 * 1024
        ),
        cost_estimate=pl.CostEstimate(flops=10**7, bytes_accessed=10**6, transcendentals=10**5),
    )(
        positions.reshape(3, 1, atom_count),
        velocity.reshape(3, 1, atom_count),
        atom_eps.reshape(1, atom_count),
        neighbours.reshape(slots, atom_count),
        pair_live.reshape(slots, atom_count),
        event_count.reshape(1, 1),
        event_atoms.reshape(events, template),
        event_weight.reshape(1, events),
        template_map,
    )
    return tuple(out.reshape(positions.shape) for out in outs)


def solution(mesh):
    in_specs = (
        P(None, "gx", "gy", "gz", None),
        P(None, "gx", "gy", "gz", None),
        P("gx", "gy", "gz", None),
        P("gx", "gy", "gz", None, None),
        P("gx", "gy", "gz", None, None),
        P("gx", "gy", "gz"),
        P("gx", "gy", "gz", None, None),
        P("gx", "gy", "gz", None),
        P(),
    )
    out_specs = (P(None, "gx", "gy", "gz", None), P(None, "gx", "gy", "gz", None))
    mesh_shape = tuple(mesh.shape[axis] for axis in ("gx", "gy", "gz"))
    return jax.shard_map(
        functools.partial(shards, mesh_shape),
        mesh=mesh,
        in_specs=in_specs,
        out_specs=out_specs,
        check_vma=False,
    )
```

```python
import functools

import jax
import jax.numpy as jnp
from jax import lax
from jax.experimental import pallas as pl
from jax.experimental.pallas import tpu as pltpu
from jax.sharding import PartitionSpec as P

width_scale = 1.5
time_step = 0.1
mixing = 0.1
epsilon = 1e-06

MESH = pl.DeviceIdType.MESH
LANES = 128
COORDS = 12
ROWS = 16
DIRECT = 64


def lane_gather(table, index):
    return jnp.take_along_axis(table, index, axis=1, mode="promise_in_bounds")


def cycle_kernel(
    mesh_shape,
    pos_in,
    vel_in,
    eps_in,
    nbr_in,
    live_in,
    atoms_in,
    weight_in,
    map_in,
    pos_out,
    vel_out,
    pos_v,
    vel_v,
    eps_v,
    nbr,
    live,
    atoms,
    tmap,
    col,
    moved,
    shifts,
    lanes_hot,
    table,
    table2,
    speeds,
    forces,
    forces2,
    sums,
    local_sem,
    col_sem,
    send_sem,
    recv_sem,
    sum_send,
    sum_recv,
):
    nx, ny, nz = mesh_shape
    devices = nx * ny * nz
    x, y, z = lax.axis_index("gx"), lax.axis_index("gy"), lax.axis_index("gz")
    slots, atom_count = nbr.shape
    events, template = atoms.shape[1:]
    chunks = atom_count // LANES
    home = 13
    depth_offsets = (0, 1) if nz == 2 else (0, 1, 2)
    depths = len(depth_offsets)

    def peer(dx, dy, dz):
        return (
            lax.rem(x + dx + nx, nx),
            lax.rem(y + dy + ny, ny),
            lax.rem(z + dz + nz, nz),
        )

    def copies(j):
        dirs = [j] if nz > 2 or j % 3 != 0 else [j, j + 2]
        return [s for d in dirs for s in range(d, slots, 27)]

    around = [
        (a, b, c)
        for a in range(3)
        for b in range(3)
        for c in depth_offsets
        if (a, b, c) != (1, 1, 1)
    ]
    beside = [(a, b) for a in range(3) for b in range(3) if (a, b) != (1, 1)]
    if devices <= DIRECT:
        stages = [
            [
                (dx, dy, dz)
                for dx in range(nx)
                for dy in range(ny)
                for dz in range(nz)
                if (dx, dy, dz) != (0, 0, 0)
            ]
        ]
    else:
        stages = [
            [(d, 0, 0) for d in range(1, nx)],
            [(0, d, 0) for d in range(1, ny)],
            [(0, 0, d) for d in range(1, nz)],
        ]
    greeted = {((1 - a) % nx, (1 - b) % ny, (1 - c) % nz) for a, b, c in around}
    greeted |= {((a - 1) % nx, (b - 1) % ny, (c - 1) % nz) for a, b, c in around}
    greeted |= {offset for stage in stages for offset in stage}
    greeted |= {(0, 0, d) for d in range(1, nz)}
    greeted = sorted(greeted)

    own_atoms = atoms.at[z]
    pairs = [
        (pos_in, pos_v),
        (vel_in, vel_v),
        (eps_in, eps_v),
        (weight_in, col.at[z, pl.ds(ROWS, weight_in.shape[0])]),
        (atoms_in, own_atoms),
        (map_in, tmap),
        (nbr_in, nbr),
        (live_in, live),
    ]
    loads = [
        pltpu.make_async_copy(src, dst, local_sem.at[i]) for i, (src, dst) in enumerate(pairs)
    ]
    for load in loads:
        load.start()
    barrier = pltpu.get_barrier_semaphore()
    for offset in greeted:
        pl.semaphore_signal(barrier, inc=1, device_id=peer(*offset), device_id_type=MESH)
    for load in loads[:5]:
        load.wait()

    for chunk in range(chunks):
        lanes = pl.ds(chunk * LANES, LANES)
        for i in range(3):
            row = i * chunks + chunk
            col[z, pl.ds(row, 1), :] = pos_v[i, :, lanes]
            speeds[pl.ds(home * ROWS + row, 1), :] = vel_v[i, :, lanes]
        row = 3 * chunks + chunk
        col[z, pl.ds(row, 1), :] = jnp.sqrt(eps_v[:, lanes])
        speeds[pl.ds(home * ROWS + row, 1), :] = col[z, pl.ds(row, 1), :]
    pl.semaphore_wait(barrier, len(greeted))

    column_copies = []
    for d in range(1, nz):
        for part, ref in enumerate((col, atoms)):
            copy = pltpu.make_async_remote_copy(
                src_ref=ref.at[z],
                dst_ref=ref.at[z],
                send_sem=col_sem.at[0, part, d - 1],
                recv_sem=col_sem.at[1, part, d - 1],
                device_id=peer(0, 0, d),
                device_id_type=MESH,
            )
            copy.start()
            column_copies.append(copy)

    def send_around(ref, rows, which):
        for a, b, c in around:
            j = (a * 3 + b) * 3 + c
            pltpu.make_async_remote_copy(
                src_ref=ref.at[pl.ds(home * ROWS, rows)],
                dst_ref=ref.at[pl.ds(j * ROWS, rows)],
                send_sem=send_sem.at[which],
                recv_sem=recv_sem.at[which],
                device_id=peer(1 - a, 1 - b, 1 - c),
                device_id_type=MESH,
            ).start()

    def wait_total(ref, rows, sem):
        part = ref.at[pl.ds(0, rows)]
        pltpu.make_async_copy(part, part, sem).wait()

    send_around(speeds, ROWS, 0)
    for load in loads[5:]:
        load.wait()

    lane_row = lax.broadcasted_iota(jnp.int32, (LANES, template), 0)
    domains = [lax.rem(z + d, nz) for d in range(nz)]

    def lane_factor(domain):
        member_lane = atoms[domain] & (LANES - 1)
        for e in range(events):
            hot = jnp.where(member_lane[e : e + 1] == lane_row, 1.0, 0.0)
            lanes_hot[domain, :, pl.ds(e * template, template)] = hot.astype(jnp.bfloat16)

    lane_factor(z)
    for d in range(1, nz):
        column_copies[2 * d - 1].wait_recv()
        lane_factor(lax.rem(z - d + nz, nz))
    for d in range(1, nz):
        column_copies[2 * d - 2].wait_recv()

    members = jnp.concatenate([atoms[domain] for domain in domains], axis=0)
    weights = jnp.concatenate([col[domain, pl.ds(ROWS, events), :] for domain in domains], axis=0)
    total_events = nz * events
    member_chunk = lax.shift_right_logical(members, 7)
    member_lane = members & (LANES - 1)
    centred = []
    for i in range(3):
        taken = jnp.zeros((total_events, template), jnp.float32)
        for d in range(nz):
            for chunk in range(chunks):
                source = jnp.broadcast_to(
                    col[d, pl.ds(i * chunks + chunk, 1), :], (total_events, LANES)
                )
                picked = lane_gather(source, member_lane)
                taken = jnp.where(member_chunk == d * chunks + chunk, picked, taken)
        mean = jnp.sum(taken, axis=1, keepdims=True) * (1.0 / template)
        centred.append(taken - mean)
    shifted = jnp.dot(
        jnp.concatenate(centred, axis=0),
        tmap[...],
        precision=lax.Precision.HIGHEST,
        preferred_element_type=jnp.float32,
    )
    for i in range(3):
        shift = shifted[i * total_events : (i + 1) * total_events] * weights
        coarse = shift.astype(jnp.bfloat16).astype(jnp.float32)
        shifts[i] = coarse
        shifts[3 + i] = shift - coarse

    column_chunks = nz * chunks
    chunk_row = lax.broadcasted_iota(jnp.int32, (column_chunks, template), 0)
    summed = jnp.zeros((6 * column_chunks, LANES), jnp.float32)
    for d, domain in enumerate(domains):
        for first in range(0, events, 2):
            left = []
            for e in range(d * events + first, d * events + first + 2):
                here = member_chunk[e : e + 1] == chunk_row
                parts = [jnp.where(here, shifts[q, pl.ds(e, 1), :], 0.0) for q in range(6)]
                left.append(jnp.concatenate(parts, axis=0))
            summed = summed + lax.dot_general(
                jnp.concatenate(left, axis=1).astype(jnp.bfloat16),
                lanes_hot[domain, :, pl.ds(first * template, 2 * template)],
                (((1,), (1,)), ((), ())),
                preferred_element_type=jnp.float32,
            )
    half = 3 * column_chunks
    displaced = summed[:half] + summed[half:]
    for d in range(nz):
        pieces = [
            displaced[i * column_chunks + d * chunks : i * column_chunks + (d + 1) * chunks]
            for i in range(3)
        ]
        pieces.append(jnp.zeros((chunks, LANES), jnp.float32))
        moved[d] = col[d, pl.ds(0, ROWS), :] + jnp.concatenate(pieces, axis=0)

    for c in range(3):
        table[pl.ds((home - 1 + c) * ROWS, ROWS), :] = moved[lax.rem(z + c - 1 + nz, nz)]
    for a, b in beside:
        for c in depth_offsets:
            pltpu.make_async_remote_copy(
                src_ref=table.at[pl.ds((home - 1 + c) * ROWS, COORDS)],
                dst_ref=table.at[pl.ds(((a * 3 + b) * 3 + c) * ROWS, COORDS)],
                send_sem=send_sem.at[1],
                recv_sem=recv_sem.at[1],
                device_id=peer(1 - a, 1 - b, 0),
                device_id_type=MESH,
            ).start()
    wait_total(speeds, len(around) * ROWS, recv_sem.at[0])
    for a, b, c in around + [(1, 1, 1)]:
        j = (a * 3 + b) * 3 + c
        for s in copies(j)[1:]:
            strengths = pl.ds(s * ROWS + COORDS, ROWS - COORDS)
            speeds[strengths, :] = speeds[pl.ds(j * ROWS + COORDS, ROWS - COORDS), :]
    wait_total(table, len(beside) * depths * COORDS, recv_sem.at[1])
    for a, b in beside:
        for c in depth_offsets:
            j = (a * 3 + b) * 3 + c
            for s in copies(j)[1:]:
                table[pl.ds(s * ROWS, COORDS), :] = table[pl.ds(j * ROWS, COORDS), :]
    for c in range(3):
        j = home - 1 + c
        for s in range(j + 27, slots, 27):
            table[pl.ds(s * ROWS, COORDS), :] = table[pl.ds(j * ROWS, COORDS), :]

    def pair_forces(where, result):
        total = [[jnp.zeros((8, LANES), jnp.float32)] * 3 for _ in range(chunks)]
        for group in range(slots // 8):
            source = [
                [
                    (where if i < 3 else speeds)[
                        pl.ds(group * 8 * ROWS + i * chunks + t, 8, stride=ROWS), :
                    ]
                    for t in range(chunks)
                ]
                for i in range(4)
            ]
            for chunk in range(chunks):
                rows, lanes = pl.ds(group * 8, 8), pl.ds(chunk * LANES, LANES)
                index = nbr[rows, lanes]
                lane, part = index & (LANES - 1), lax.shift_right_logical(index, 7)
                partner = []
                for i in range(4):
                    picked = lane_gather(source[i][0], lane)
                    for t in range(1, chunks):
                        picked = jnp.where(part == t, lane_gather(source[i][t], lane), picked)
                    partner.append(picked)
                own = [
                    (where if i < 3 else speeds)[pl.ds(home * ROWS + i * chunks + chunk, 1), :]
                    for i in range(4)
                ]
                apart = [own[i] - partner[i] for i in range(3)]
                square = apart[0] * apart[0] + apart[1] * apart[1] + apart[2] * apart[2]
                strength = (
                    own[3]
                    * partner[3]
                    * live[rows, lanes].astype(jnp.float32)
                    * jnp.exp(square * (-0.5 / (width_scale * width_scale)))
                    * (1.0 / (width_scale * width_scale))
                )
                total[chunk] = [total[chunk][i] + strength * apart[i] for i in range(3)]
        for chunk in range(chunks):
            for i in range(3):
                result[pl.ds(home * ROWS + i * chunks + chunk, 1), :] = jnp.sum(
                    total[chunk][i], axis=0, keepdims=True
                )

    def whole(value):
        return jnp.sum(jnp.sum(value, axis=0, keepdims=True), axis=1, keepdims=True)

    lane_index = lax.broadcasted_iota(jnp.int32, (1, LANES), 1)
    most = max(len(stage) for stage in stages) + 1

    def sum_start(force, speed, which):
        row = jnp.where(lane_index == 0, whole(force * speed), 0.0)
        row = jnp.where(lane_index == 1, whole(speed * speed), row)
        row = jnp.where(lane_index == 2, whole(force * force), row)
        return stage_start(row, which, 0)

    def stage_start(row, which, s):
        base = (which * len(stages) + s) * most
        sums[base] = row
        for slot, offset in enumerate(stages[s]):
            pltpu.make_async_remote_copy(
                src_ref=sums.at[base],
                dst_ref=sums.at[base + 1 + slot],
                send_sem=sum_send.at[which, s],
                recv_sem=sum_recv.at[which, s],
                device_id=peer(*offset),
                device_id_type=MESH,
            ).start()

    def sum_finish(which):
        for s, stage in enumerate(stages):
            base = (which * len(stages) + s) * most
            wait_total(sums, len(stage), sum_recv.at[which, s])
            row = jnp.sum(sums[pl.ds(base, len(stage) + 1)], axis=0)
            if s + 1 < len(stages):
                stage_start(row, which, s + 1)
        power, speed_sq, force_sq = row[:, 0:1], row[:, 1:2], row[:, 2:3]
        cosine = power / (jnp.sqrt(speed_sq + epsilon) * jnp.sqrt(force_sq + epsilon))
        ratio = jnp.sqrt((speed_sq + epsilon) / (force_sq + epsilon))
        keep = 0.5 * (1.0 + cosine)
        return keep * (1.0 - mixing), keep * mixing * ratio + time_step

    def block(ref, j):
        return ref[pl.ds(j * ROWS, COORDS), :]

    pair_forces(table, forces)
    send_around(forces, COORDS, 2)
    sum_start(block(forces, home), block(speeds, home), 0)
    old, new = sum_finish(0)
    wait_total(forces, len(around) * COORDS, recv_sem.at[2])
    for a, b, c in around + [(1, 1, 1)]:
        j = (a * 3 + b) * 3 + c
        later = block(table, j) + time_step * (
            old * block(speeds, j) + new * block(forces, j)
        )
        for s in copies(j):
            table2[pl.ds(s * ROWS, COORDS), :] = later
    speed = old * block(speeds, home) + new * block(forces, home)

    pair_forces(table2, forces2)
    force = block(forces2, home)
    sum_start(force, speed, 1)
    old, new = sum_finish(1)
    speed = old * speed + new * force
    place = block(table2, home) + time_step * speed
    for chunk in range(chunks):
        lanes = pl.ds(chunk * LANES, LANES)
        for i in range(3):
            row = i * chunks + chunk
            pos_out[i, :, lanes] = place[row : row + 1]
            vel_out[i, :, lanes] = speed[row : row + 1]

    for copy in column_copies:
        copy.wait_send()
    wait_total(speeds, len(around) * ROWS, send_sem.at[0])
    wait_total(table, len(beside) * depths * COORDS, send_sem.at[1])
    wait_total(forces, len(around) * COORDS, send_sem.at[2])
    for which in range(2):
        for s, stage in enumerate(stages):
            wait_total(sums, len(stage), sum_send.at[which, s])


def shards(
    mesh_shape,
    positions,
    velocity,
    atom_eps,
    neighbours,
    pair_live,
    event_count,
    event_atoms,
    event_weight,
    template_map,
):
    atom_count = positions.shape[4]
    slots = neighbours.shape[3]
    events, template = event_atoms.shape[3:]
    nx, ny, nz = mesh_shape
    devices = nx * ny * nz
    stages, most = (1, devices) if devices <= DIRECT else (3, max(mesh_shape))
    alive = jnp.arange(events, dtype=jnp.int32) < event_count.reshape(())
    live_weights = jnp.where(alive, event_weight.reshape(events), 0.0)
    live_weights = jnp.broadcast_to(live_weights[:, None], (events, LANES))
    f32, i32 = jnp.float32, jnp.int32
    blocks = pltpu.VMEM((slots * ROWS, LANES), f32)
    outs = pl.pallas_call(
        functools.partial(cycle_kernel, mesh_shape),
        out_shape=[jax.ShapeDtypeStruct((3, 1, atom_count), f32)] * 2,
        in_specs=[pl.BlockSpec(memory_space=pltpu.HBM)] * 8,
        out_specs=[pl.BlockSpec(memory_space=pltpu.VMEM)] * 2,
        scratch_shapes=[
            pltpu.VMEM((3, 1, atom_count), f32),
            pltpu.VMEM((3, 1, atom_count), f32),
            pltpu.VMEM((1, atom_count), f32),
            pltpu.VMEM((slots, atom_count), i32),
            pltpu.VMEM((slots, atom_count), i32),
            pltpu.VMEM((nz, events, template), i32),
            pltpu.VMEM((template, template), f32),
            pltpu.VMEM((nz, ROWS + events, LANES), f32),
            pltpu.VMEM((nz, ROWS, LANES), f32),
            pltpu.VMEM((6, nz * events, template), f32),
            pltpu.VMEM((nz, LANES, events * template), jnp.bfloat16),
            blocks,
            blocks,
            blocks,
            blocks,
            blocks,
            pltpu.VMEM((2 * stages * most, 1, LANES), f32),
            pltpu.SemaphoreType.DMA((8,)),
            pltpu.SemaphoreType.DMA((2, 2, nz - 1)),
            pltpu.SemaphoreType.DMA((3,)),
            pltpu.SemaphoreType.DMA((3,)),
            pltpu.SemaphoreType.DMA((2, stages)),
            pltpu.SemaphoreType.DMA((2, stages)),
        ],
        compiler_params=pltpu.CompilerParams(
            collective_id=0, has_side_effects=True, vmem_limit_bytes=60 * 1024 * 1024
        ),
        cost_estimate=pl.CostEstimate(flops=10**7, bytes_accessed=10**6, transcendentals=10**5),
    )(
        positions.reshape(3, 1, atom_count),
        velocity.reshape(3, 1, atom_count),
        atom_eps.reshape(1, atom_count),
        neighbours.reshape(slots, atom_count),
        pair_live.reshape(slots, atom_count),
        event_atoms.reshape(events, template),
        live_weights,
        template_map,
    )
    return tuple(out.reshape(positions.shape) for out in outs)


def solution(mesh):
    in_specs = (
        P(None, "gx", "gy", "gz", None),
        P(None, "gx", "gy", "gz", None),
        P("gx", "gy", "gz", None),
        P("gx", "gy", "gz", None, None),
        P("gx", "gy", "gz", None, None),
        P("gx", "gy", "gz"),
        P("gx", "gy", "gz", None, None),
        P("gx", "gy", "gz", None),
        P(),
    )
    out_specs = (P(None, "gx", "gy", "gz", None), P(None, "gx", "gy", "gz", None))
    mesh_shape = tuple(mesh.shape[axis] for axis in ("gx", "gy", "gz"))
    return jax.shard_map(
        functools.partial(shards, mesh_shape),
        mesh=mesh,
        in_specs=in_specs,
        out_specs=out_specs,
        check_vma=False,
    )
```

```python
import functools

import jax
import jax.numpy as jnp
from jax import lax
from jax.experimental import pallas as pl
from jax.experimental.pallas import tpu as pltpu
from jax.sharding import PartitionSpec as P

width_scale = 1.5
time_step = 0.1
mixing = 0.1
epsilon = 1e-06

MESH = pl.DeviceIdType.MESH
LANES = 128
COORDS = 12
ROWS = 16
NEAR = 8


def lane_gather(table, index):
    return jnp.take_along_axis(table, index, axis=1, mode="promise_in_bounds")


def sum_stages(mesh_shape):
    nx, ny, nz = mesh_shape
    if nx * nz <= NEAR:
        first = [[(dx, 0, dz) for dx in range(nx) for dz in range(nz) if (dx, dz) != (0, 0)]]
    else:
        first = [[(d, 0, 0) for d in range(1, nx)], [(0, 0, d) for d in range(1, nz)]]
    return first + [[(0, d, 0) for d in range(1, ny)]]


def cycle_kernel(
    mesh_shape,
    pos_in,
    vel_in,
    eps_in,
    nbr_in,
    live_in,
    count_in,
    atoms_in,
    weight_in,
    map_in,
    pos_out,
    vel_out,
    pos_v,
    vel_v,
    eps_v,
    nbr,
    live,
    atoms,
    weight_v,
    tmap,
    col,
    moved,
    shifts,
    lanes_hot,
    table,
    table2,
    speeds,
    forces,
    forces2,
    sums,
    local_sem,
    col_sem,
    send_sem,
    recv_sem,
    sum_send,
    sum_recv,
):
    nx, ny, nz = mesh_shape
    x, y, z = lax.axis_index("gx"), lax.axis_index("gy"), lax.axis_index("gz")
    slots, atom_count = nbr.shape
    events, template = atoms.shape[1:]
    chunks = atom_count // LANES
    home = 13
    depth_offsets = (0, 1) if nz == 2 else (0, 1, 2)
    depths = len(depth_offsets)

    def peer(dx, dy, dz):
        return (
            lax.rem(x + dx + nx, nx),
            lax.rem(y + dy + ny, ny),
            lax.rem(z + dz + nz, nz),
        )

    def copies(j):
        dirs = [j] if nz > 2 or j % 3 != 0 else [j, j + 2]
        return [s for d in dirs for s in range(d, slots, 27)]

    around = [
        (a, b, c)
        for a in range(3)
        for b in range(3)
        for c in depth_offsets
        if (a, b, c) != (1, 1, 1)
    ]
    beside = [(a, b) for a in range(3) for b in range(3) if (a, b) != (1, 1)]
    stages = sum_stages(mesh_shape)
    greeted = {((1 - a) % nx, (1 - b) % ny, (1 - c) % nz) for a, b, c in around}
    greeted |= {((a - 1) % nx, (b - 1) % ny, (c - 1) % nz) for a, b, c in around}
    greeted |= {offset for stage in stages for offset in stage}
    greeted |= {(0, 0, d) for d in range(1, nz)}
    greeted = sorted(greeted)

    own_atoms = atoms.at[z]
    pairs = [
        (pos_in, pos_v),
        (vel_in, vel_v),
        (eps_in, eps_v),
        (weight_in, weight_v),
        (atoms_in, own_atoms),
        (map_in, tmap),
        (nbr_in, nbr),
        (live_in, live),
    ]
    loads = [
        pltpu.make_async_copy(src, dst, local_sem.at[i]) for i, (src, dst) in enumerate(pairs)
    ]
    for load in loads:
        load.start()
    barrier = pltpu.get_barrier_semaphore()
    for offset in greeted:
        pl.semaphore_signal(barrier, inc=1, device_id=peer(*offset), device_id_type=MESH)
    for load in loads[:5]:
        load.wait()

    for chunk in range(chunks):
        lanes = pl.ds(chunk * LANES, LANES)
        for i in range(3):
            row = i * chunks + chunk
            col[z, pl.ds(row, 1), :] = pos_v[i, :, lanes]
            speeds[pl.ds(home * ROWS + row, 1), :] = vel_v[i, :, lanes]
        row = 3 * chunks + chunk
        col[z, pl.ds(row, 1), :] = jnp.sqrt(eps_v[:, lanes])
        speeds[pl.ds(home * ROWS + row, 1), :] = col[z, pl.ds(row, 1), :]
    alive = lax.broadcasted_iota(jnp.int32, (1, events), 1) < count_in[0, 0, 0]
    spread = jnp.broadcast_to(jnp.where(alive, weight_v[...], 0.0), (events, events))
    diagonal = lax.broadcasted_iota(jnp.int32, (events, events), 0) == lax.broadcasted_iota(
        jnp.int32, (events, events), 1
    )
    column_weight = jnp.sum(jnp.where(diagonal, spread, 0.0), axis=1, keepdims=True)
    col[z, pl.ds(ROWS, events), :] = jnp.broadcast_to(column_weight, (events, LANES))

    pl.semaphore_wait(barrier, len(greeted))

    column_copies = []
    for d in range(1, nz):
        for part, ref in enumerate((col, atoms)):
            copy = pltpu.make_async_remote_copy(
                src_ref=ref.at[z],
                dst_ref=ref.at[z],
                send_sem=col_sem.at[0, part, d - 1],
                recv_sem=col_sem.at[1, part, d - 1],
                device_id=peer(0, 0, d),
                device_id_type=MESH,
            )
            copy.start()
            column_copies.append(copy)

    def send_around(ref, rows, which):
        for a, b, c in around:
            j = (a * 3 + b) * 3 + c
            pltpu.make_async_remote_copy(
                src_ref=ref.at[pl.ds(home * ROWS, rows)],
                dst_ref=ref.at[pl.ds(j * ROWS, rows)],
                send_sem=send_sem.at[which],
                recv_sem=recv_sem.at[which],
                device_id=peer(1 - a, 1 - b, 1 - c),
                device_id_type=MESH,
            ).start()

    def wait_total(ref, rows, sem):
        part = ref.at[pl.ds(0, rows)]
        pltpu.make_async_copy(part, part, sem).wait()

    send_around(speeds, ROWS, 0)
    for load in loads[5:]:
        load.wait()

    lane_row = lax.broadcasted_iota(jnp.int32, (LANES, template), 0)
    domains = [lax.rem(z + d, nz) for d in range(nz)]

    def lane_factor(domain):
        member_lane = atoms[domain] & (LANES - 1)
        for e in range(events):
            hot = jnp.where(member_lane[e : e + 1] == lane_row, 1.0, 0.0)
            lanes_hot[domain, :, pl.ds(e * template, template)] = hot.astype(jnp.bfloat16)

    lane_factor(z)
    for d in range(1, nz):
        column_copies[2 * d - 1].wait_recv()
        lane_factor(lax.rem(z - d + nz, nz))
    for d in range(1, nz):
        column_copies[2 * d - 2].wait_recv()

    members = jnp.concatenate([atoms[domain] for domain in domains], axis=0)
    weights = jnp.concatenate([col[domain, pl.ds(ROWS, events), :] for domain in domains], axis=0)
    total_events = nz * events
    member_chunk = lax.shift_right_logical(members, 7)
    member_lane = members & (LANES - 1)
    centred = []
    for i in range(3):
        taken = jnp.zeros((total_events, template), jnp.float32)
        for d in range(nz):
            for chunk in range(chunks):
                source = jnp.broadcast_to(
                    col[d, pl.ds(i * chunks + chunk, 1), :], (total_events, LANES)
                )
                picked = lane_gather(source, member_lane)
                taken = jnp.where(member_chunk == d * chunks + chunk, picked, taken)
        mean = jnp.sum(taken, axis=1, keepdims=True) * (1.0 / template)
        centred.append(taken - mean)
    shifted = jnp.dot(
        jnp.concatenate(centred, axis=0),
        tmap[...],
        precision=lax.Precision.HIGHEST,
        preferred_element_type=jnp.float32,
    )
    for i in range(3):
        shift = shifted[i * total_events : (i + 1) * total_events] * weights
        coarse = shift.astype(jnp.bfloat16).astype(jnp.float32)
        shifts[i] = coarse
        shifts[3 + i] = shift - coarse

    column_chunks = nz * chunks
    chunk_row = lax.broadcasted_iota(jnp.int32, (column_chunks, template), 0)
    summed = jnp.zeros((6 * column_chunks, LANES), jnp.float32)
    for d, domain in enumerate(domains):
        for first in range(0, events, 2):
            left = []
            for e in range(d * events + first, d * events + first + 2):
                here = member_chunk[e : e + 1] == chunk_row
                parts = [jnp.where(here, shifts[q, pl.ds(e, 1), :], 0.0) for q in range(6)]
                left.append(jnp.concatenate(parts, axis=0))
            summed = summed + lax.dot_general(
                jnp.concatenate(left, axis=1).astype(jnp.bfloat16),
                lanes_hot[domain, :, pl.ds(first * template, 2 * template)],
                (((1,), (1,)), ((), ())),
                preferred_element_type=jnp.float32,
            )
    half = 3 * column_chunks
    displaced = summed[:half] + summed[half:]
    for d in range(nz):
        pieces = [
            displaced[i * column_chunks + d * chunks : i * column_chunks + (d + 1) * chunks]
            for i in range(3)
        ]
        pieces.append(jnp.zeros((chunks, LANES), jnp.float32))
        moved[d] = col[d, pl.ds(0, ROWS), :] + jnp.concatenate(pieces, axis=0)

    def place_of(slot, count=1):
        return pl.ds(slot * COORDS, count * COORDS)

    for c in range(3):
        table[place_of(home - 1 + c), :] = moved[lax.rem(z + c - 1 + nz, nz), pl.ds(0, COORDS), :]
    for a, b in beside:
        pltpu.make_async_remote_copy(
            src_ref=table.at[place_of(home - 1, depths)],
            dst_ref=table.at[place_of((a * 3 + b) * 3, depths)],
            send_sem=send_sem.at[1],
            recv_sem=recv_sem.at[1],
            device_id=peer(1 - a, 1 - b, 0),
            device_id_type=MESH,
        ).start()
    wait_total(speeds, len(around) * ROWS, recv_sem.at[0])
    for a, b, c in around + [(1, 1, 1)]:
        j = (a * 3 + b) * 3 + c
        for s in copies(j)[1:]:
            strengths = pl.ds(s * ROWS + COORDS, ROWS - COORDS)
            speeds[strengths, :] = speeds[pl.ds(j * ROWS + COORDS, ROWS - COORDS), :]
    wait_total(table, len(beside) * depths * COORDS, recv_sem.at[1])
    for a, b in beside:
        for c in depth_offsets:
            j = (a * 3 + b) * 3 + c
            for s in copies(j)[1:]:
                table[place_of(s), :] = table[place_of(j), :]
    for c in range(3):
        j = home - 1 + c
        for s in range(j + 27, slots, 27):
            table[place_of(s), :] = table[place_of(j), :]

    def pair_forces(where, result):
        total = [[jnp.zeros((8, LANES), jnp.float32)] * 3 for _ in range(chunks)]
        for group in range(slots // 8):
            source = [
                [
                    where[pl.ds(group * 8 * COORDS + i * chunks + t, 8, stride=COORDS), :]
                    if i < 3
                    else speeds[pl.ds(group * 8 * ROWS + i * chunks + t, 8, stride=ROWS), :]
                    for t in range(chunks)
                ]
                for i in range(4)
            ]
            for chunk in range(chunks):
                rows, lanes = pl.ds(group * 8, 8), pl.ds(chunk * LANES, LANES)
                index = nbr[rows, lanes]
                lane, part = index & (LANES - 1), lax.shift_right_logical(index, 7)
                partner = []
                for i in range(4):
                    picked = lane_gather(source[i][0], lane)
                    for t in range(1, chunks):
                        picked = jnp.where(part == t, lane_gather(source[i][t], lane), picked)
                    partner.append(picked)
                own = [
                    where[pl.ds(home * COORDS + i * chunks + chunk, 1), :] for i in range(3)
                ]
                own.append(speeds[pl.ds(home * ROWS + COORDS + chunk, 1), :])
                apart = [own[i] - partner[i] for i in range(3)]
                square = apart[0] * apart[0] + apart[1] * apart[1] + apart[2] * apart[2]
                strength = (
                    own[3]
                    * partner[3]
                    * live[rows, lanes].astype(jnp.float32)
                    * jnp.exp(square * (-0.5 / (width_scale * width_scale)))
                    * (1.0 / (width_scale * width_scale))
                )
                total[chunk] = [total[chunk][i] + strength * apart[i] for i in range(3)]
        for chunk in range(chunks):
            for i in range(3):
                result[pl.ds(home * ROWS + i * chunks + chunk, 1), :] = jnp.sum(
                    total[chunk][i], axis=0, keepdims=True
                )

    most = max(len(stage) for stage in stages) + 1

    def fold(value):
        return jnp.sum(value, axis=0, keepdims=True)

    def sum_start(force, speed, which):
        rows = [fold(force * speed), fold(speed * speed), fold(force * force)]
        rows.append(jnp.zeros((5, LANES), jnp.float32))
        return stage_start(jnp.concatenate(rows, axis=0), which, 0)

    def stage_start(row, which, s):
        base = (which * len(stages) + s) * most
        sums[base] = row
        for slot, offset in enumerate(stages[s]):
            pltpu.make_async_remote_copy(
                src_ref=sums.at[base],
                dst_ref=sums.at[base + 1 + slot],
                send_sem=sum_send.at[which, s],
                recv_sem=sum_recv.at[which, s],
                device_id=peer(*offset),
                device_id_type=MESH,
            ).start()

    def sum_finish(which):
        for s, stage in enumerate(stages):
            base = (which * len(stages) + s) * most
            wait_total(sums, len(stage), sum_recv.at[which, s])
            row = jnp.sum(sums[pl.ds(base, len(stage) + 1)], axis=0)
            if s + 1 < len(stages):
                stage_start(row, which, s + 1)
        total = jnp.sum(row, axis=1, keepdims=True)
        power, speed_sq, force_sq = total[0:1], total[1:2], total[2:3]
        cosine = power / (jnp.sqrt(speed_sq + epsilon) * jnp.sqrt(force_sq + epsilon))
        ratio = jnp.sqrt((speed_sq + epsilon) / (force_sq + epsilon))
        keep = 0.5 * (1.0 + cosine)
        return keep * (1.0 - mixing), keep * mixing * ratio + time_step

    def block(ref, j):
        return ref[pl.ds(j * ROWS, COORDS), :]

    pair_forces(table, forces)
    sum_start(block(forces, home), block(speeds, home), 0)
    send_around(forces, COORDS, 2)
    old, new = sum_finish(0)
    wait_total(forces, len(around) * COORDS, recv_sem.at[2])
    for a, b, c in around + [(1, 1, 1)]:
        j = (a * 3 + b) * 3 + c
        later = table[place_of(j), :] + time_step * (
            old * block(speeds, j) + new * block(forces, j)
        )
        for s in copies(j):
            table2[place_of(s), :] = later
    speed = old * block(speeds, home) + new * block(forces, home)

    pair_forces(table2, forces2)
    force = block(forces2, home)
    sum_start(force, speed, 1)
    old, new = sum_finish(1)
    speed = old * speed + new * force
    place = table2[place_of(home), :] + time_step * speed
    for chunk in range(chunks):
        lanes = pl.ds(chunk * LANES, LANES)
        for i in range(3):
            row = i * chunks + chunk
            pos_v[i, :, lanes] = place[row : row + 1]
            vel_v[i, :, lanes] = speed[row : row + 1]
    stores = [
        pltpu.make_async_copy(pos_v, pos_out, local_sem.at[0]),
        pltpu.make_async_copy(vel_v, vel_out, local_sem.at[1]),
    ]
    for store in stores:
        store.start()

    for copy in column_copies:
        copy.wait_send()
    wait_total(speeds, len(around) * ROWS, send_sem.at[0])
    wait_total(table, len(beside) * depths * COORDS, send_sem.at[1])
    wait_total(forces, len(around) * COORDS, send_sem.at[2])
    for which in range(2):
        for s, stage in enumerate(stages):
            wait_total(sums, len(stage), sum_send.at[which, s])
    for store in stores:
        store.wait()


def hand_over(pos, vel, pos_out, vel_out, sem):
    both = [
        pltpu.make_async_copy(src, dst, sem.at[i])
        for i, (src, dst) in enumerate(((pos, pos_out), (vel, vel_out)))
    ]
    for copy in both:
        copy.start()
    for copy in both:
        copy.wait()


def shards(
    mesh_shape,
    positions,
    velocity,
    atom_eps,
    neighbours,
    pair_live,
    event_count,
    event_atoms,
    event_weight,
    template_map,
):
    atom_count = positions.shape[4]
    slots = neighbours.shape[3]
    events, template = event_atoms.shape[3:]
    nz = mesh_shape[2]
    stages = len(sum_stages(mesh_shape))
    most = max(len(stage) for stage in sum_stages(mesh_shape)) + 1
    f32, i32 = jnp.float32, jnp.int32
    blocks = pltpu.VMEM((slots * ROWS, LANES), f32)
    outs = pl.pallas_call(
        functools.partial(cycle_kernel, mesh_shape),
        out_shape=[jax.ShapeDtypeStruct((3, 1, atom_count), f32)] * 2,
        in_specs=[pl.BlockSpec(memory_space=pltpu.HBM)] * 5
        + [pl.BlockSpec(memory_space=pltpu.SMEM)]
        + [pl.BlockSpec(memory_space=pltpu.HBM)] * 3,
        out_specs=[pl.BlockSpec(memory_space=pl.ANY)] * 2,
        scratch_shapes=[
            pltpu.VMEM((3, 1, atom_count), f32),
            pltpu.VMEM((3, 1, atom_count), f32),
            pltpu.VMEM((1, atom_count), f32),
            pltpu.VMEM((slots, atom_count), i32),
            pltpu.VMEM((slots, atom_count), i32),
            pltpu.VMEM((nz, events, template), i32),
            pltpu.VMEM((1, events), f32),
            pltpu.VMEM((template, template), f32),
            pltpu.VMEM((nz, ROWS + events, LANES), f32),
            pltpu.VMEM((nz, ROWS, LANES), f32),
            pltpu.VMEM((6, nz * events, template), f32),
            pltpu.VMEM((nz, LANES, events * template), jnp.bfloat16),
            pltpu.VMEM((slots * COORDS, LANES), f32),
            pltpu.VMEM((slots * COORDS, LANES), f32),
            blocks,
            blocks,
            blocks,
            pltpu.VMEM((2 * stages * most, 8, LANES), f32),
            pltpu.SemaphoreType.DMA((8,)),
            pltpu.SemaphoreType.DMA((2, 2, nz - 1)),
            pltpu.SemaphoreType.DMA((3,)),
            pltpu.SemaphoreType.DMA((3,)),
            pltpu.SemaphoreType.DMA((2, stages)),
            pltpu.SemaphoreType.DMA((2, stages)),
        ],
        compiler_params=pltpu.CompilerParams(
            collective_id=0, has_side_effects=True, vmem_limit_bytes=60 * 1024 * 1024
        ),
        cost_estimate=pl.CostEstimate(flops=10**7, bytes_accessed=10**6, transcendentals=10**5),
    )(
        positions.reshape(3, 1, atom_count),
        velocity.reshape(3, 1, atom_count),
        atom_eps.reshape(1, atom_count),
        neighbours.reshape(slots, atom_count),
        pair_live.reshape(slots, atom_count),
        event_count,
        event_atoms.reshape(events, template),
        event_weight.reshape(1, events),
        template_map,
    )
    results = pl.pallas_call(
        hand_over,
        out_shape=[jax.ShapeDtypeStruct((3, 1, atom_count), f32)] * 2,
        in_specs=[pl.BlockSpec(memory_space=pl.ANY)] * 2,
        out_specs=[pl.BlockSpec(memory_space=pl.ANY)] * 2,
        scratch_shapes=[pltpu.SemaphoreType.DMA((2,))],
        compiler_params=pltpu.CompilerParams(vmem_limit_bytes=60 * 1024 * 1024),
    )(*outs)
    return tuple(result.reshape(positions.shape) for result in results)


def solution(mesh):
    in_specs = (
        P(None, "gx", "gy", "gz", None),
        P(None, "gx", "gy", "gz", None),
        P("gx", "gy", "gz", None),
        P("gx", "gy", "gz", None, None),
        P("gx", "gy", "gz", None, None),
        P("gx", "gy", "gz"),
        P("gx", "gy", "gz", None, None),
        P("gx", "gy", "gz", None),
        P(),
    )
    out_specs = (P(None, "gx", "gy", "gz", None), P(None, "gx", "gy", "gz", None))
    mesh_shape = tuple(mesh.shape[axis] for axis in ("gx", "gy", "gz"))
    return jax.shard_map(
        functools.partial(shards, mesh_shape),
        mesh=mesh,
        in_specs=in_specs,
        out_specs=out_specs,
        check_vma=False,
    )
```

```python
import functools

import jax
import jax.numpy as jnp
from jax import lax
from jax.experimental import pallas as pl
from jax.experimental.pallas import tpu as pltpu
from jax.sharding import PartitionSpec as P

width_scale = 1.5
time_step = 0.1
mixing = 0.1
epsilon = 1e-06

MESH = pl.DeviceIdType.MESH
LANES = 128
COORDS = 12
ROWS = 16
DIRECT = 64


def lane_gather(table, index):
    return jnp.take_along_axis(table, index, axis=1, mode="promise_in_bounds")


def sum_stages(mesh_shape):
    nx, ny, nz = mesh_shape
    if nx >= 3 and ny >= 3 and nx * ny * nz <= DIRECT:
        every = [(dx, dy, dz) for dx in range(nx) for dy in range(ny) for dz in range(nz)]
        return [sorted(every[1:], key=lambda offset: -sum(map(bool, offset)))]
    return [
        [(d, 0, 0) for d in range(1, nx)],
        [(0, 0, d) for d in range(1, nz)],
        [(0, d, 0) for d in range(1, ny)],
    ]


def cycle_kernel(
    mesh_shape,
    pos_in,
    vel_in,
    eps_in,
    nbr_in,
    live_in,
    count_in,
    atoms_in,
    weight_in,
    map_in,
    pos_out,
    vel_out,
    pos_v,
    vel_v,
    eps_v,
    nbr,
    live,
    atoms,
    weight_v,
    tmap,
    col,
    moved,
    shifts,
    lanes_hot,
    table,
    table2,
    speeds,
    forces,
    forces2,
    sums,
    local_sem,
    col_sem,
    send_sem,
    recv_sem,
    sum_send,
    sum_recv,
):
    nx, ny, nz = mesh_shape
    x, y, z = lax.axis_index("gx"), lax.axis_index("gy"), lax.axis_index("gz")
    slots, atom_count = nbr.shape
    events, template = atoms.shape[1:]
    chunks = atom_count // LANES
    home = 13
    depth_offsets = (0, 1) if nz == 2 else (0, 1, 2)
    depths = len(depth_offsets)

    def peer(dx, dy, dz):
        return (
            lax.rem(x + dx + nx, nx),
            lax.rem(y + dy + ny, ny),
            lax.rem(z + dz + nz, nz),
        )

    def copies(j):
        dirs = [j] if nz > 2 or j % 3 != 0 else [j, j + 2]
        return [s for d in dirs for s in range(d, slots, 27)]

    around = [
        (a, b, c)
        for a in range(3)
        for b in range(3)
        for c in depth_offsets
        if (a, b, c) != (1, 1, 1)
    ]
    around.sort(key=lambda direction: -sum(d != 1 for d in direction))
    beside = [(a, b) for a in range(3) for b in range(3) if (a, b) != (1, 1)]
    beside.sort(key=lambda direction: -sum(d != 1 for d in direction))
    stages = sum_stages(mesh_shape)
    direct = len(stages) == 1
    near = {((1 - a) % nx, (1 - b) % ny, (1 - c) % nz) for a, b, c in around}
    alone = [[offset for offset in stages[0] if offset not in near]] if direct else stages
    greeted = {((1 - a) % nx, (1 - b) % ny, (1 - c) % nz) for a, b, c in around}
    greeted |= {((a - 1) % nx, (b - 1) % ny, (c - 1) % nz) for a, b, c in around}
    greeted |= {offset for stage in stages for offset in stage}
    greeted |= {(0, 0, d) for d in range(1, nz)}
    greeted = sorted(greeted)

    barrier = pltpu.get_barrier_semaphore()
    for offset in greeted:
        pl.semaphore_signal(barrier, inc=1, device_id=peer(*offset), device_id_type=MESH)

    own_atoms = atoms.at[z]
    pairs = [
        (pos_in, pos_v),
        (vel_in, vel_v),
        (eps_in, eps_v),
        (weight_in, weight_v),
        (atoms_in, own_atoms),
        (map_in, tmap),
        (nbr_in, nbr),
        (live_in, live),
    ]
    loads = [
        pltpu.make_async_copy(src, dst, local_sem.at[i]) for i, (src, dst) in enumerate(pairs)
    ]
    for load in loads:
        load.start()
    for load in loads[:5]:
        load.wait()

    for chunk in range(chunks):
        lanes = pl.ds(chunk * LANES, LANES)
        for i in range(3):
            row = i * chunks + chunk
            col[z, pl.ds(row, 1), :] = pos_v[i, :, lanes]
            speeds[pl.ds(home * ROWS + row, 1), :] = vel_v[i, :, lanes]
        row = 3 * chunks + chunk
        col[z, pl.ds(row, 1), :] = jnp.sqrt(eps_v[:, lanes])
        speeds[pl.ds(home * ROWS + row, 1), :] = col[z, pl.ds(row, 1), :]
    alive = lax.broadcasted_iota(jnp.int32, (1, events), 1) < count_in[0, 0, 0]
    spread = jnp.broadcast_to(jnp.where(alive, weight_v[...], 0.0), (events, events))
    diagonal = lax.broadcasted_iota(jnp.int32, (events, events), 0) == lax.broadcasted_iota(
        jnp.int32, (events, events), 1
    )
    column_weight = jnp.sum(jnp.where(diagonal, spread, 0.0), axis=1, keepdims=True)
    col[z, pl.ds(ROWS, events), :] = jnp.broadcast_to(column_weight, (events, LANES))

    lane_row = lax.broadcasted_iota(jnp.int32, (LANES, template), 0)
    domains = [lax.rem(z + d, nz) for d in range(nz)]

    def lane_factor(domain):
        member_lane = atoms[domain] & (LANES - 1)
        for e in range(events):
            hot = jnp.where(member_lane[e : e + 1] == lane_row, 1.0, 0.0)
            lanes_hot[domain, :, pl.ds(e * template, template)] = hot.astype(jnp.bfloat16)

    lane_factor(z)
    pl.semaphore_wait(barrier, len(greeted))

    column_copies = []
    for d in range(1, nz):
        for part, ref in enumerate((col, atoms)):
            copy = pltpu.make_async_remote_copy(
                src_ref=ref.at[z],
                dst_ref=ref.at[z],
                send_sem=col_sem.at[0, part, d - 1],
                recv_sem=col_sem.at[1, part, d - 1],
                device_id=peer(0, 0, d),
                device_id_type=MESH,
            )
            copy.start()
            column_copies.append(copy)

    def send_around(ref, rows, which):
        for a, b, c in around:
            j = (a * 3 + b) * 3 + c
            pltpu.make_async_remote_copy(
                src_ref=ref.at[pl.ds(home * ROWS, rows)],
                dst_ref=ref.at[pl.ds(j * ROWS, rows)],
                send_sem=send_sem.at[which],
                recv_sem=recv_sem.at[which],
                device_id=peer(1 - a, 1 - b, 1 - c),
                device_id_type=MESH,
            ).start()

    def wait_total(ref, rows, sem):
        part = ref.at[pl.ds(0, rows)]
        pltpu.make_async_copy(part, part, sem).wait()

    send_around(speeds, ROWS, 0)
    for load in loads[5:]:
        load.wait()

    for d in range(1, nz):
        column_copies[2 * d - 1].wait_recv()
        lane_factor(lax.rem(z - d + nz, nz))
    for d in range(1, nz):
        column_copies[2 * d - 2].wait_recv()

    members = jnp.concatenate([atoms[domain] for domain in domains], axis=0)
    weights = jnp.concatenate([col[domain, pl.ds(ROWS, events), :] for domain in domains], axis=0)
    total_events = nz * events
    member_chunk = lax.shift_right_logical(members, 7)
    member_lane = members & (LANES - 1)
    centred = []
    for i in range(3):
        taken = jnp.zeros((total_events, template), jnp.float32)
        for d in range(nz):
            for chunk in range(chunks):
                source = jnp.broadcast_to(
                    col[d, pl.ds(i * chunks + chunk, 1), :], (total_events, LANES)
                )
                picked = lane_gather(source, member_lane)
                taken = jnp.where(member_chunk == d * chunks + chunk, picked, taken)
        mean = jnp.sum(taken, axis=1, keepdims=True) * (1.0 / template)
        centred.append(taken - mean)
    shifted = jnp.dot(
        jnp.concatenate(centred, axis=0),
        tmap[...],
        precision=lax.Precision.HIGHEST,
        preferred_element_type=jnp.float32,
    )
    for i in range(3):
        shift = shifted[i * total_events : (i + 1) * total_events] * weights
        coarse = shift.astype(jnp.bfloat16).astype(jnp.float32)
        shifts[i] = coarse
        shifts[3 + i] = shift - coarse

    column_chunks = nz * chunks
    chunk_row = lax.broadcasted_iota(jnp.int32, (column_chunks, template), 0)
    summed = jnp.zeros((6 * column_chunks, LANES), jnp.float32)
    for d, domain in enumerate(domains):
        for first in range(0, events, 2):
            left = []
            for e in range(d * events + first, d * events + first + 2):
                here = member_chunk[e : e + 1] == chunk_row
                parts = [jnp.where(here, shifts[q, pl.ds(e, 1), :], 0.0) for q in range(6)]
                left.append(jnp.concatenate(parts, axis=0))
            summed = summed + lax.dot_general(
                jnp.concatenate(left, axis=1).astype(jnp.bfloat16),
                lanes_hot[domain, :, pl.ds(first * template, 2 * template)],
                (((1,), (1,)), ((), ())),
                preferred_element_type=jnp.float32,
            )
    half = 3 * column_chunks
    displaced = summed[:half] + summed[half:]
    for d in range(nz):
        pieces = [
            displaced[i * column_chunks + d * chunks : i * column_chunks + (d + 1) * chunks]
            for i in range(3)
        ]
        pieces.append(jnp.zeros((chunks, LANES), jnp.float32))
        moved[d] = col[d, pl.ds(0, ROWS), :] + jnp.concatenate(pieces, axis=0)

    def place_of(slot, count=1):
        return pl.ds(slot * COORDS, count * COORDS)

    for c in range(3):
        table[place_of(home - 1 + c), :] = moved[lax.rem(z + c - 1 + nz, nz), pl.ds(0, COORDS), :]
    for a, b in beside:
        pltpu.make_async_remote_copy(
            src_ref=table.at[place_of(home - 1, depths)],
            dst_ref=table.at[place_of((a * 3 + b) * 3, depths)],
            send_sem=send_sem.at[1],
            recv_sem=recv_sem.at[1],
            device_id=peer(1 - a, 1 - b, 0),
            device_id_type=MESH,
        ).start()
    wait_total(speeds, len(around) * ROWS, recv_sem.at[0])
    for a, b, c in around + [(1, 1, 1)]:
        j = (a * 3 + b) * 3 + c
        for s in copies(j)[1:]:
            strengths = pl.ds(s * ROWS + COORDS, ROWS - COORDS)
            speeds[strengths, :] = speeds[pl.ds(j * ROWS + COORDS, ROWS - COORDS), :]
    wait_total(table, len(beside) * depths * COORDS, recv_sem.at[1])
    for a, b in beside:
        for c in depth_offsets:
            j = (a * 3 + b) * 3 + c
            for s in copies(j)[1:]:
                table[place_of(s), :] = table[place_of(j), :]
    for c in range(3):
        j = home - 1 + c
        for s in range(j + 27, slots, 27):
            table[place_of(s), :] = table[place_of(j), :]

    def pair_forces(where, result):
        total = [[jnp.zeros((8, LANES), jnp.float32)] * 3 for _ in range(chunks)]
        for group in range(slots // 8):
            source = [
                [
                    where[pl.ds(group * 8 * COORDS + i * chunks + t, 8, stride=COORDS), :]
                    if i < 3
                    else speeds[pl.ds(group * 8 * ROWS + i * chunks + t, 8, stride=ROWS), :]
                    for t in range(chunks)
                ]
                for i in range(4)
            ]
            for chunk in range(chunks):
                rows, lanes = pl.ds(group * 8, 8), pl.ds(chunk * LANES, LANES)
                index = nbr[rows, lanes]
                lane, part = index & (LANES - 1), lax.shift_right_logical(index, 7)
                partner = []
                for i in range(4):
                    picked = lane_gather(source[i][0], lane)
                    for t in range(1, chunks):
                        picked = jnp.where(part == t, lane_gather(source[i][t], lane), picked)
                    partner.append(picked)
                own = [
                    where[pl.ds(home * COORDS + i * chunks + chunk, 1), :] for i in range(3)
                ]
                own.append(speeds[pl.ds(home * ROWS + COORDS + chunk, 1), :])
                apart = [own[i] - partner[i] for i in range(3)]
                square = apart[0] * apart[0] + apart[1] * apart[1] + apart[2] * apart[2]
                strength = (
                    own[3]
                    * partner[3]
                    * live[rows, lanes].astype(jnp.float32)
                    * jnp.exp(square * (-0.5 / (width_scale * width_scale)))
                    * (1.0 / (width_scale * width_scale))
                )
                total[chunk] = [total[chunk][i] + strength * apart[i] for i in range(3)]
        for chunk in range(chunks):
            for i in range(3):
                result[pl.ds(home * ROWS + i * chunks + chunk, 1), :] = jnp.sum(
                    total[chunk][i], axis=0, keepdims=True
                )

    most = max(len(stage) for stage in stages) + 1

    def fold(value):
        return jnp.sum(value, axis=0, keepdims=True)

    def sum_rows(force, speed):
        rows = [fold(force * speed), fold(speed * speed), fold(force * force)]
        return jnp.concatenate(rows + [jnp.zeros((1, LANES), jnp.float32)], axis=0)

    def stage_start(row, which, s):
        base = (which * len(stages) + s) * most
        sums[base] = row
        for slot, offset in enumerate((alone, stages)[which][s]):
            pltpu.make_async_remote_copy(
                src_ref=sums.at[base],
                dst_ref=sums.at[base + 1 + slot],
                send_sem=sum_send.at[which, s],
                recv_sem=sum_recv.at[which, s],
                device_id=peer(*offset),
                device_id_type=MESH,
            ).start()

    def sum_finish(which):
        for s, stage in enumerate((alone, stages)[which]):
            base = (which * len(stages) + s) * most
            if stage:
                wait_total(sums, len(stage), sum_recv.at[which, s])
            row = jnp.sum(sums[pl.ds(base, len(stage) + 1)], axis=0)
            if s + 1 < len(stages):
                stage_start(row, which, s + 1)
        if which == 0:
            wait_total(forces, len(around) * ROWS, recv_sem.at[2])
            if direct:
                for a, b, c in around:
                    j = (a * 3 + b) * 3 + c
                    row = row + forces[pl.ds(j * ROWS + COORDS, ROWS - COORDS), :]
        total = jnp.sum(row, axis=1, keepdims=True)
        power, speed_sq, force_sq = total[0:1], total[1:2], total[2:3]
        cosine = power / (jnp.sqrt(speed_sq + epsilon) * jnp.sqrt(force_sq + epsilon))
        ratio = jnp.sqrt((speed_sq + epsilon) / (force_sq + epsilon))
        keep = 0.5 * (1.0 + cosine)
        return keep * (1.0 - mixing), keep * mixing * ratio + time_step

    def block(ref, j):
        return ref[pl.ds(j * ROWS, COORDS), :]

    pair_forces(table, forces)
    row = sum_rows(block(forces, home), block(speeds, home))
    forces[pl.ds(home * ROWS + COORDS, ROWS - COORDS), :] = row
    send_around(forces, ROWS, 2)
    stage_start(row, 0, 0)
    old, new = sum_finish(0)
    for a, b, c in around + [(1, 1, 1)]:
        j = (a * 3 + b) * 3 + c
        later = table[place_of(j), :] + time_step * (
            old * block(speeds, j) + new * block(forces, j)
        )
        for s in copies(j):
            table2[place_of(s), :] = later
    speed = old * block(speeds, home) + new * block(forces, home)

    pair_forces(table2, forces2)
    force = block(forces2, home)
    stage_start(sum_rows(force, speed), 1, 0)
    old, new = sum_finish(1)
    speed = old * speed + new * force
    place = table2[place_of(home), :] + time_step * speed
    for chunk in range(chunks):
        lanes = pl.ds(chunk * LANES, LANES)
        for i in range(3):
            row = i * chunks + chunk
            pos_v[i, :, lanes] = place[row : row + 1]
            vel_v[i, :, lanes] = speed[row : row + 1]
    stores = [
        pltpu.make_async_copy(pos_v, pos_out, local_sem.at[0]),
        pltpu.make_async_copy(vel_v, vel_out, local_sem.at[1]),
    ]
    for store in stores:
        store.start()

    for copy in column_copies:
        copy.wait_send()
    wait_total(speeds, len(around) * ROWS, send_sem.at[0])
    wait_total(table, len(beside) * depths * COORDS, send_sem.at[1])
    wait_total(forces, len(around) * ROWS, send_sem.at[2])
    for which in range(2):
        for s, stage in enumerate((alone, stages)[which]):
            if stage:
                wait_total(sums, len(stage), sum_send.at[which, s])
    for store in stores:
        store.wait()


def hand_over(pos, vel, pos_out, vel_out, sem):
    both = [
        pltpu.make_async_copy(src, dst, sem.at[i])
        for i, (src, dst) in enumerate(((pos, pos_out), (vel, vel_out)))
    ]
    for copy in both:
        copy.start()
    for copy in both:
        copy.wait()


def shards(
    mesh_shape,
    positions,
    velocity,
    atom_eps,
    neighbours,
    pair_live,
    event_count,
    event_atoms,
    event_weight,
    template_map,
):
    atom_count = positions.shape[4]
    slots = neighbours.shape[3]
    events, template = event_atoms.shape[3:]
    nz = mesh_shape[2]
    stages = len(sum_stages(mesh_shape))
    most = max(len(stage) for stage in sum_stages(mesh_shape)) + 1
    f32, i32 = jnp.float32, jnp.int32
    blocks = pltpu.VMEM((slots * ROWS, LANES), f32)
    outs = pl.pallas_call(
        functools.partial(cycle_kernel, mesh_shape),
        out_shape=[jax.ShapeDtypeStruct((3, 1, atom_count), f32)] * 2,
        in_specs=[pl.BlockSpec(memory_space=pltpu.HBM)] * 5
        + [pl.BlockSpec(memory_space=pltpu.SMEM)]
        + [pl.BlockSpec(memory_space=pltpu.HBM)] * 3,
        out_specs=[pl.BlockSpec(memory_space=pl.ANY)] * 2,
        scratch_shapes=[
            pltpu.VMEM((3, 1, atom_count), f32),
            pltpu.VMEM((3, 1, atom_count), f32),
            pltpu.VMEM((1, atom_count), f32),
            pltpu.VMEM((slots, atom_count), i32),
            pltpu.VMEM((slots, atom_count), i32),
            pltpu.VMEM((nz, events, template), i32),
            pltpu.VMEM((1, events), f32),
            pltpu.VMEM((template, template), f32),
            pltpu.VMEM((nz, ROWS + events, LANES), f32),
            pltpu.VMEM((nz, ROWS, LANES), f32),
            pltpu.VMEM((6, nz * events, template), f32),
            pltpu.VMEM((nz, LANES, events * template), jnp.bfloat16),
            pltpu.VMEM((slots * COORDS, LANES), f32),
            pltpu.VMEM((slots * COORDS, LANES), f32),
            blocks,
            blocks,
            blocks,
            pltpu.VMEM((2 * stages * most, 4, LANES), f32),
            pltpu.SemaphoreType.DMA((8,)),
            pltpu.SemaphoreType.DMA((2, 2, nz - 1)),
            pltpu.SemaphoreType.DMA((3,)),
            pltpu.SemaphoreType.DMA((3,)),
            pltpu.SemaphoreType.DMA((2, stages)),
            pltpu.SemaphoreType.DMA((2, stages)),
        ],
        compiler_params=pltpu.CompilerParams(
            collective_id=0, has_side_effects=True, vmem_limit_bytes=60 * 1024 * 1024
        ),
        cost_estimate=pl.CostEstimate(flops=10**7, bytes_accessed=10**6, transcendentals=10**5),
    )(
        positions.reshape(3, 1, atom_count),
        velocity.reshape(3, 1, atom_count),
        atom_eps.reshape(1, atom_count),
        neighbours.reshape(slots, atom_count),
        pair_live.reshape(slots, atom_count),
        event_count,
        event_atoms.reshape(events, template),
        event_weight.reshape(1, events),
        template_map,
    )
    results = pl.pallas_call(
        hand_over,
        out_shape=[jax.ShapeDtypeStruct((3, 1, atom_count), f32)] * 2,
        in_specs=[pl.BlockSpec(memory_space=pl.ANY)] * 2,
        out_specs=[pl.BlockSpec(memory_space=pl.ANY)] * 2,
        scratch_shapes=[pltpu.SemaphoreType.DMA((2,))],
        compiler_params=pltpu.CompilerParams(vmem_limit_bytes=60 * 1024 * 1024),
    )(*outs)
    return tuple(result.reshape(positions.shape) for result in results)


def solution(mesh):
    in_specs = (
        P(None, "gx", "gy", "gz", None),
        P(None, "gx", "gy", "gz", None),
        P("gx", "gy", "gz", None),
        P("gx", "gy", "gz", None, None),
        P("gx", "gy", "gz", None, None),
        P("gx", "gy", "gz"),
        P("gx", "gy", "gz", None, None),
        P("gx", "gy", "gz", None),
        P(),
    )
    out_specs = (P(None, "gx", "gy", "gz", None), P(None, "gx", "gy", "gz", None))
    mesh_shape = tuple(mesh.shape[axis] for axis in ("gx", "gy", "gz"))
    return jax.shard_map(
        functools.partial(shards, mesh_shape),
        mesh=mesh,
        in_specs=in_specs,
        out_specs=out_specs,
        check_vma=False,
    )
```

```python
import functools

import jax
import jax.numpy as jnp
from jax import lax
from jax.experimental import pallas as pl
from jax.experimental.pallas import tpu as pltpu
from jax.sharding import PartitionSpec as P

width_scale = 1.5
time_step = 0.1
mixing = 0.1
epsilon = 1e-06

MESH = pl.DeviceIdType.MESH
LANES = 128
COORDS = 12
ROWS = 16
DIRECT = 64


def lane_gather(table, index):
    return jnp.take_along_axis(table, index, axis=1, mode="promise_in_bounds")


def sum_stages(mesh_shape):
    nx, ny, nz = mesh_shape
    if nx >= 3 and ny >= 3 and nx * ny * nz <= DIRECT:
        every = [(dx, dy, dz) for dx in range(nx) for dy in range(ny) for dz in range(nz)]
        return [sorted(every[1:], key=lambda offset: -sum(map(bool, offset)))]
    return [
        [(d, 0, 0) for d in range(1, nx)],
        [(0, 0, d) for d in range(1, nz)],
        [(0, d, 0) for d in range(1, ny)],
    ]


def cycle_kernel(
    mesh_shape,
    pos_in,
    vel_in,
    eps_in,
    nbr_in,
    live_in,
    count_in,
    atoms_in,
    weight_in,
    map_in,
    pos_out,
    vel_out,
    pos_v,
    vel_v,
    eps_v,
    nbr,
    live,
    atoms,
    weight_v,
    tmap,
    col,
    moved,
    shifts,
    lanes_hot,
    table,
    table2,
    speeds,
    forces,
    forces2,
    sums,
    local_sem,
    col_sem,
    send_sem,
    recv_sem,
    sum_send,
    sum_recv,
):
    nx, ny, nz = mesh_shape
    x, y, z = lax.axis_index("gx"), lax.axis_index("gy"), lax.axis_index("gz")
    slots, atom_count = nbr.shape
    events, template = atoms.shape[1:]
    chunks = atom_count // LANES
    home = 13
    depth_offsets = (0, 1) if nz == 2 else (0, 1, 2)
    depths = len(depth_offsets)

    def peer(dx, dy, dz):
        return (
            lax.rem(x + dx + nx, nx),
            lax.rem(y + dy + ny, ny),
            lax.rem(z + dz + nz, nz),
        )

    def copies(j):
        dirs = [j] if nz > 2 or j % 3 != 0 else [j, j + 2]
        return [s for d in dirs for s in range(d, slots, 27)]

    around = [
        (a, b, c)
        for a in range(3)
        for b in range(3)
        for c in depth_offsets
        if (a, b, c) != (1, 1, 1)
    ]
    around.sort(key=lambda direction: -sum(d != 1 for d in direction))
    beside = [(a, b) for a in range(3) for b in range(3) if (a, b) != (1, 1)]
    beside.sort(key=lambda direction: -sum(d != 1 for d in direction))
    stages = sum_stages(mesh_shape)
    direct = len(stages) == 1
    near = {((1 - a) % nx, (1 - b) % ny, (1 - c) % nz) for a, b, c in around}
    alone = [[offset for offset in stages[0] if offset not in near]] if direct else stages
    greeted = {((1 - a) % nx, (1 - b) % ny, (1 - c) % nz) for a, b, c in around}
    greeted |= {((a - 1) % nx, (b - 1) % ny, (c - 1) % nz) for a, b, c in around}
    greeted |= {offset for stage in stages for offset in stage}
    greeted |= {(0, 0, d) for d in range(1, nz)}
    greeted = sorted(greeted)

    barrier = pltpu.get_barrier_semaphore()
    for offset in greeted:
        pl.semaphore_signal(barrier, inc=1, device_id=peer(*offset), device_id_type=MESH)

    own_atoms = atoms.at[z]
    pairs = [
        (pos_in, pos_v),
        (vel_in, vel_v),
        (eps_in, eps_v),
        (weight_in, weight_v),
        (atoms_in, own_atoms),
        (map_in, tmap),
        (nbr_in, nbr),
        (live_in, live),
    ]
    loads = [
        pltpu.make_async_copy(src, dst, local_sem.at[i]) for i, (src, dst) in enumerate(pairs)
    ]
    for load in loads:
        load.start()
    for load in loads[:5]:
        load.wait()

    for chunk in range(chunks):
        lanes = pl.ds(chunk * LANES, LANES)
        for i in range(3):
            row = i * chunks + chunk
            col[z, pl.ds(row, 1), :] = pos_v[i, :, lanes]
            speeds[pl.ds(home * ROWS + row, 1), :] = vel_v[i, :, lanes]
        row = 3 * chunks + chunk
        col[z, pl.ds(row, 1), :] = jnp.sqrt(eps_v[:, lanes])
        speeds[pl.ds(home * ROWS + row, 1), :] = col[z, pl.ds(row, 1), :]
    alive = lax.broadcasted_iota(jnp.int32, (1, events), 1) < count_in[0, 0, 0]
    spread = jnp.broadcast_to(jnp.where(alive, weight_v[...], 0.0), (events, events))
    diagonal = lax.broadcasted_iota(jnp.int32, (events, events), 0) == lax.broadcasted_iota(
        jnp.int32, (events, events), 1
    )
    column_weight = jnp.sum(jnp.where(diagonal, spread, 0.0), axis=1, keepdims=True)
    col[z, pl.ds(ROWS, events), :] = jnp.broadcast_to(column_weight, (events, LANES))

    lane_row = lax.broadcasted_iota(jnp.int32, (LANES, template), 0)
    domains = [lax.rem(z + d, nz) for d in range(nz)]

    def lane_factor(domain):
        member_lane = atoms[domain] & (LANES - 1)
        for e in range(events):
            hot = jnp.where(member_lane[e : e + 1] == lane_row, 1.0, 0.0)
            lanes_hot[domain, :, pl.ds(e * template, template)] = hot.astype(jnp.bfloat16)

    pl.semaphore_wait(barrier, len(greeted))

    column_copies = []
    for d in range(1, nz):
        for part, ref in enumerate((col, atoms)):
            copy = pltpu.make_async_remote_copy(
                src_ref=ref.at[z],
                dst_ref=ref.at[z],
                send_sem=col_sem.at[0, part, d - 1],
                recv_sem=col_sem.at[1, part, d - 1],
                device_id=peer(0, 0, d),
                device_id_type=MESH,
            )
            copy.start()
            column_copies.append(copy)

    def send_around(ref, rows, which):
        for a, b, c in around:
            j = (a * 3 + b) * 3 + c
            pltpu.make_async_remote_copy(
                src_ref=ref.at[pl.ds(home * ROWS, rows)],
                dst_ref=ref.at[pl.ds(j * ROWS, rows)],
                send_sem=send_sem.at[which],
                recv_sem=recv_sem.at[which],
                device_id=peer(1 - a, 1 - b, 1 - c),
                device_id_type=MESH,
            ).start()

    def wait_total(ref, rows, sem):
        part = ref.at[pl.ds(0, rows)]
        pltpu.make_async_copy(part, part, sem).wait()

    send_around(speeds, ROWS, 0)
    for load in loads[5:]:
        load.wait()

    lane_factor(z)
    for d in range(1, nz):
        column_copies[2 * d - 1].wait_recv()
        lane_factor(lax.rem(z - d + nz, nz))
    for d in range(1, nz):
        column_copies[2 * d - 2].wait_recv()

    members = jnp.concatenate([atoms[domain] for domain in domains], axis=0)
    weights = jnp.concatenate([col[domain, pl.ds(ROWS, events), :] for domain in domains], axis=0)
    total_events = nz * events
    member_chunk = lax.shift_right_logical(members, 7)
    member_lane = members & (LANES - 1)
    centred = []
    for i in range(3):
        taken = jnp.zeros((total_events, template), jnp.float32)
        for d in range(nz):
            for chunk in range(chunks):
                source = jnp.broadcast_to(
                    col[d, pl.ds(i * chunks + chunk, 1), :], (total_events, LANES)
                )
                picked = lane_gather(source, member_lane)
                taken = jnp.where(member_chunk == d * chunks + chunk, picked, taken)
        mean = jnp.sum(taken, axis=1, keepdims=True) * (1.0 / template)
        centred.append(taken - mean)
    shifted = jnp.dot(
        jnp.concatenate(centred, axis=0),
        tmap[...],
        precision=lax.Precision.HIGHEST,
        preferred_element_type=jnp.float32,
    )
    for i in range(3):
        shift = shifted[i * total_events : (i + 1) * total_events] * weights
        coarse = shift.astype(jnp.bfloat16).astype(jnp.float32)
        shifts[i] = coarse
        shifts[3 + i] = shift - coarse

    column_chunks = nz * chunks
    chunk_row = lax.broadcasted_iota(jnp.int32, (column_chunks, template), 0)
    summed = jnp.zeros((6 * column_chunks, LANES), jnp.float32)
    for d, domain in enumerate(domains):
        for first in range(0, events, 2):
            left = []
            for e in range(d * events + first, d * events + first + 2):
                here = member_chunk[e : e + 1] == chunk_row
                parts = [jnp.where(here, shifts[q, pl.ds(e, 1), :], 0.0) for q in range(6)]
                left.append(jnp.concatenate(parts, axis=0))
            summed = summed + lax.dot_general(
                jnp.concatenate(left, axis=1).astype(jnp.bfloat16),
                lanes_hot[domain, :, pl.ds(first * template, 2 * template)],
                (((1,), (1,)), ((), ())),
                preferred_element_type=jnp.float32,
            )
    half = 3 * column_chunks
    displaced = summed[:half] + summed[half:]
    for d in range(nz):
        pieces = [
            displaced[i * column_chunks + d * chunks : i * column_chunks + (d + 1) * chunks]
            for i in range(3)
        ]
        pieces.append(jnp.zeros((chunks, LANES), jnp.float32))
        moved[d] = col[d, pl.ds(0, ROWS), :] + jnp.concatenate(pieces, axis=0)

    def place_of(slot):
        return pl.ds(slot * ROWS, COORDS)

    for c in range(3):
        table[place_of(home - 1 + c), :] = moved[lax.rem(z + c - 1 + nz, nz), pl.ds(0, COORDS), :]
    for a, b in beside:
        for c in depth_offsets:
            pltpu.make_async_remote_copy(
                src_ref=table.at[place_of(home - 1 + c)],
                dst_ref=table.at[place_of((a * 3 + b) * 3 + c)],
                send_sem=send_sem.at[1],
                recv_sem=recv_sem.at[1],
                device_id=peer(1 - a, 1 - b, 0),
                device_id_type=MESH,
            ).start()
    wait_total(speeds, len(around) * ROWS, recv_sem.at[0])
    for a, b, c in around + [(1, 1, 1)]:
        j = (a * 3 + b) * 3 + c
        for s in copies(j)[1:]:
            strengths = pl.ds(s * ROWS + COORDS, ROWS - COORDS)
            speeds[strengths, :] = speeds[pl.ds(j * ROWS + COORDS, ROWS - COORDS), :]
    wait_total(table, len(beside) * depths * COORDS, recv_sem.at[1])
    for a, b in beside:
        for c in depth_offsets:
            j = (a * 3 + b) * 3 + c
            for s in copies(j)[1:]:
                table[place_of(s), :] = table[place_of(j), :]
    for c in range(3):
        j = home - 1 + c
        for s in range(j + 27, slots, 27):
            table[place_of(s), :] = table[place_of(j), :]

    def pair_forces(where, result):
        total = [[jnp.zeros((8, LANES), jnp.float32)] * 3 for _ in range(chunks)]
        for group in range(slots // 8):
            source = [
                [
                    (where if i < 3 else speeds)[
                        pl.ds(group * 8 * ROWS + i * chunks + t, 8, stride=ROWS), :
                    ]
                    for t in range(chunks)
                ]
                for i in range(4)
            ]
            for chunk in range(chunks):
                rows, lanes = pl.ds(group * 8, 8), pl.ds(chunk * LANES, LANES)
                index = nbr[rows, lanes]
                lane, part = index & (LANES - 1), lax.shift_right_logical(index, 7)
                partner = []
                for i in range(4):
                    picked = lane_gather(source[i][0], lane)
                    for t in range(1, chunks):
                        picked = jnp.where(part == t, lane_gather(source[i][t], lane), picked)
                    partner.append(picked)
                own = [
                    where[pl.ds(home * ROWS + i * chunks + chunk, 1), :] for i in range(3)
                ]
                own.append(speeds[pl.ds(home * ROWS + COORDS + chunk, 1), :])
                apart = [own[i] - partner[i] for i in range(3)]
                square = apart[0] * apart[0] + apart[1] * apart[1] + apart[2] * apart[2]
                strength = (
                    own[3]
                    * partner[3]
                    * live[rows, lanes].astype(jnp.float32)
                    * jnp.exp(square * (-0.5 / (width_scale * width_scale)))
                    * (1.0 / (width_scale * width_scale))
                )
                total[chunk] = [total[chunk][i] + strength * apart[i] for i in range(3)]
        for chunk in range(chunks):
            for i in range(3):
                result[pl.ds(home * ROWS + i * chunks + chunk, 1), :] = jnp.sum(
                    total[chunk][i], axis=0, keepdims=True
                )

    most = max(len(stage) for stage in stages) + 1

    def fold(value):
        return jnp.sum(value, axis=0, keepdims=True)

    lane_index = lax.broadcasted_iota(jnp.int32, (1, LANES), 1)

    def sum_row(force, speed):
        parts = [fold(force * speed), fold(speed * speed), fold(force * force)]
        power, speed_sq, force_sq = [jnp.sum(part, axis=1, keepdims=True) for part in parts]
        row = jnp.where(lane_index == 0, power, jnp.where(lane_index == 1, speed_sq, 0.0))
        return jnp.where(lane_index == 2, force_sq, row)

    def stage_start(row, which, s):
        base = (which * len(stages) + s) * most
        sums[base] = row
        for slot, offset in enumerate((alone, stages)[which][s]):
            pltpu.make_async_remote_copy(
                src_ref=sums.at[base],
                dst_ref=sums.at[base + 1 + slot],
                send_sem=sum_send.at[which, s],
                recv_sem=sum_recv.at[which, s],
                device_id=peer(*offset),
                device_id_type=MESH,
            ).start()

    def sum_finish(which):
        for s, stage in enumerate((alone, stages)[which]):
            base = (which * len(stages) + s) * most
            if stage:
                wait_total(sums, len(stage), sum_recv.at[which, s])
            row = jnp.sum(sums[pl.ds(base, len(stage) + 1)], axis=0)
            if s + 1 < len(stages):
                stage_start(row, which, s + 1)
        if which == 0:
            wait_total(forces, len(around) * (COORDS + 1), recv_sem.at[2])
            if direct:
                for a, b, c in around:
                    j = (a * 3 + b) * 3 + c
                    row = row + forces[pl.ds(j * ROWS + COORDS, 1), :]
        power, speed_sq, force_sq = row[:, 0:1], row[:, 1:2], row[:, 2:3]
        cosine = power / (jnp.sqrt(speed_sq + epsilon) * jnp.sqrt(force_sq + epsilon))
        ratio = jnp.sqrt((speed_sq + epsilon) / (force_sq + epsilon))
        keep = 0.5 * (1.0 + cosine)
        return keep * (1.0 - mixing), keep * mixing * ratio + time_step

    def block(ref, j):
        return ref[pl.ds(j * ROWS, COORDS), :]

    pair_forces(table, forces)
    row = sum_row(block(forces, home), block(speeds, home))
    forces[pl.ds(home * ROWS + COORDS, 1), :] = row
    send_around(forces, COORDS + 1, 2)
    stage_start(row, 0, 0)
    old, new = sum_finish(0)
    for a, b, c in around + [(1, 1, 1)]:
        j = (a * 3 + b) * 3 + c
        later = table[place_of(j), :] + time_step * (
            old * block(speeds, j) + new * block(forces, j)
        )
        for s in copies(j):
            table2[place_of(s), :] = later
    speed = old * block(speeds, home) + new * block(forces, home)

    pair_forces(table2, forces2)
    force = block(forces2, home)
    stage_start(sum_row(force, speed), 1, 0)
    old, new = sum_finish(1)
    speed = old * speed + new * force
    place = table2[place_of(home), :] + time_step * speed
    for chunk in range(chunks):
        lanes = pl.ds(chunk * LANES, LANES)
        for i in range(3):
            row = i * chunks + chunk
            pos_out[i, :, lanes] = place[row : row + 1]
            vel_out[i, :, lanes] = speed[row : row + 1]
    for copy in column_copies:
        copy.wait_send()
    wait_total(speeds, len(around) * ROWS, send_sem.at[0])
    wait_total(table, len(beside) * depths * COORDS, send_sem.at[1])
    wait_total(forces, len(around) * (COORDS + 1), send_sem.at[2])
    for which in range(2):
        for s, stage in enumerate((alone, stages)[which]):
            if stage:
                wait_total(sums, len(stage), sum_send.at[which, s])


def shards(
    mesh_shape,
    positions,
    velocity,
    atom_eps,
    neighbours,
    pair_live,
    event_count,
    event_atoms,
    event_weight,
    template_map,
):
    atom_count = positions.shape[4]
    slots = neighbours.shape[3]
    events, template = event_atoms.shape[3:]
    nz = mesh_shape[2]
    stages = len(sum_stages(mesh_shape))
    most = max(len(stage) for stage in sum_stages(mesh_shape)) + 1
    f32, i32 = jnp.float32, jnp.int32
    blocks = pltpu.VMEM((slots * ROWS, LANES), f32)
    outs = pl.pallas_call(
        functools.partial(cycle_kernel, mesh_shape),
        out_shape=[jax.ShapeDtypeStruct((3, 1, atom_count), f32)] * 2,
        in_specs=[pl.BlockSpec(memory_space=pltpu.HBM)] * 5
        + [pl.BlockSpec(memory_space=pltpu.SMEM)]
        + [pl.BlockSpec(memory_space=pltpu.HBM)] * 3,
        out_specs=[pl.BlockSpec(memory_space=pltpu.VMEM)] * 2,
        scratch_shapes=[
            pltpu.VMEM((3, 1, atom_count), f32),
            pltpu.VMEM((3, 1, atom_count), f32),
            pltpu.VMEM((1, atom_count), f32),
            pltpu.VMEM((slots, atom_count), i32),
            pltpu.VMEM((slots, atom_count), i32),
            pltpu.VMEM((nz, events, template), i32),
            pltpu.VMEM((1, events), f32),
            pltpu.VMEM((template, template), f32),
            pltpu.VMEM((nz, ROWS + events, LANES), f32),
            pltpu.VMEM((nz, ROWS, LANES), f32),
            pltpu.VMEM((6, nz * events, template), f32),
            pltpu.VMEM((nz, LANES, events * template), jnp.bfloat16),
            blocks,
            blocks,
            blocks,
            blocks,
            blocks,
            pltpu.VMEM((2 * stages * most, 1, LANES), f32),
            pltpu.SemaphoreType.DMA((8,)),
            pltpu.SemaphoreType.DMA((2, 2, nz - 1)),
            pltpu.SemaphoreType.DMA((3,)),
            pltpu.SemaphoreType.DMA((3,)),
            pltpu.SemaphoreType.DMA((2, stages)),
            pltpu.SemaphoreType.DMA((2, stages)),
        ],
        compiler_params=pltpu.CompilerParams(
            collective_id=0, has_side_effects=True, vmem_limit_bytes=56520704
        ),
        cost_estimate=pl.CostEstimate(flops=10**7, bytes_accessed=10**6, transcendentals=10**5),
    )(
        positions.reshape(3, 1, atom_count),
        velocity.reshape(3, 1, atom_count),
        atom_eps.reshape(1, atom_count),
        neighbours.reshape(slots, atom_count),
        pair_live.reshape(slots, atom_count),
        event_count,
        event_atoms.reshape(events, template),
        event_weight.reshape(1, events),
        template_map,
    )
    return tuple(result.reshape(positions.shape) for result in outs)


def solution(mesh):
    in_specs = (
        P(None, "gx", "gy", "gz", None),
        P(None, "gx", "gy", "gz", None),
        P("gx", "gy", "gz", None),
        P("gx", "gy", "gz", None, None),
        P("gx", "gy", "gz", None, None),
        P("gx", "gy", "gz"),
        P("gx", "gy", "gz", None, None),
        P("gx", "gy", "gz", None),
        P(),
    )
    out_specs = (P(None, "gx", "gy", "gz", None), P(None, "gx", "gy", "gz", None))
    mesh_shape = tuple(mesh.shape[axis] for axis in ("gx", "gy", "gz"))
    return jax.shard_map(
        functools.partial(shards, mesh_shape),
        mesh=mesh,
        in_specs=in_specs,
        out_specs=out_specs,
        check_vma=False,
    )
```

```python
import functools

import jax
import jax.numpy as jnp
from jax import lax
from jax.experimental import pallas as pl
from jax.experimental.pallas import tpu as pltpu
from jax.sharding import PartitionSpec as P

width_scale = 1.5
time_step = 0.1
mixing = 0.1
epsilon = 1e-06

MESH = pl.DeviceIdType.MESH
LANES = 128
COORDS = 12
ROWS = 16
DIRECT = 64


def lane_gather(table, index):
    return jnp.take_along_axis(table, index, axis=1, mode="promise_in_bounds")


def sum_stages(mesh_shape):
    nx, ny, nz = mesh_shape
    if nx >= 3 and ny >= 3 and nx * ny * nz <= DIRECT:
        every = [(dx, dy, dz) for dx in range(nx) for dy in range(ny) for dz in range(nz)]
        return [sorted(every[1:], key=lambda offset: -sum(map(bool, offset)))]
    return [
        [(d, 0, 0) for d in range(1, nx)],
        [(0, 0, d) for d in range(1, nz)],
        [(0, d, 0) for d in range(1, ny)],
    ]


def cycle_kernel(
    mesh_shape,
    pos_in,
    vel_in,
    eps_in,
    nbr_in,
    live_in,
    count_in,
    atoms_in,
    weight_in,
    map_in,
    pos_out,
    vel_out,
    pos_v,
    vel_v,
    eps_v,
    nbr,
    live,
    atoms,
    weight_v,
    tmap,
    col,
    moved,
    shifts,
    lanes_hot,
    factor,
    table,
    table2,
    speeds,
    forces,
    forces2,
    sums,
    local_sem,
    col_sem,
    send_sem,
    recv_sem,
    sum_send,
    sum_recv,
):
    nx, ny, nz = mesh_shape
    x, y, z = lax.axis_index("gx"), lax.axis_index("gy"), lax.axis_index("gz")
    slots, atom_count = nbr.shape
    events, template = atoms.shape[1:]
    chunks = atom_count // LANES
    home = 13
    depth_offsets = (0, 1) if nz == 2 else (0, 1, 2)
    depths = len(depth_offsets)

    def peer(dx, dy, dz):
        return (
            lax.rem(x + dx + nx, nx),
            lax.rem(y + dy + ny, ny),
            lax.rem(z + dz + nz, nz),
        )

    def copies(j):
        dirs = [j] if nz > 2 or j % 3 != 0 else [j, j + 2]
        return [s for d in dirs for s in range(d, slots, 27)]

    around = [
        (a, b, c)
        for a in range(3)
        for b in range(3)
        for c in depth_offsets
        if (a, b, c) != (1, 1, 1)
    ]
    around.sort(key=lambda direction: -sum(d != 1 for d in direction))
    beside = [(a, b) for a in range(3) for b in range(3) if (a, b) != (1, 1)]
    beside.sort(key=lambda direction: -sum(d != 1 for d in direction))
    stages = sum_stages(mesh_shape)
    direct = len(stages) == 1
    near = {((1 - a) % nx, (1 - b) % ny, (1 - c) % nz) for a, b, c in around}
    alone = [[offset for offset in stages[0] if offset not in near]] if direct else stages
    greeted = {((1 - a) % nx, (1 - b) % ny, (1 - c) % nz) for a, b, c in around}
    greeted |= {((a - 1) % nx, (b - 1) % ny, (c - 1) % nz) for a, b, c in around}
    greeted |= {offset for stage in stages for offset in stage}
    greeted |= {(0, 0, d) for d in range(1, nz)}
    greeted = sorted(greeted)

    barrier = pltpu.get_barrier_semaphore()
    for offset in greeted:
        pl.semaphore_signal(barrier, inc=1, device_id=peer(*offset), device_id_type=MESH)

    own_atoms = atoms.at[z]
    pairs = [
        (pos_in, pos_v),
        (vel_in, vel_v),
        (eps_in, eps_v),
        (weight_in, weight_v),
        (atoms_in, own_atoms),
        (map_in, tmap),
        (nbr_in, nbr),
        (live_in, live),
    ]
    loads = [
        pltpu.make_async_copy(src, dst, local_sem.at[i]) for i, (src, dst) in enumerate(pairs)
    ]
    for load in loads:
        load.start()
    for load in loads[:5]:
        load.wait()

    for chunk in range(chunks):
        lanes = pl.ds(chunk * LANES, LANES)
        for i in range(3):
            row = i * chunks + chunk
            col[z, pl.ds(row, 1), :] = pos_v[i, :, lanes]
            speeds[pl.ds(home * ROWS + row, 1), :] = vel_v[i, :, lanes]
        row = 3 * chunks + chunk
        col[z, pl.ds(row, 1), :] = jnp.sqrt(eps_v[:, lanes])
        speeds[pl.ds(home * ROWS + row, 1), :] = col[z, pl.ds(row, 1), :]
    alive = lax.broadcasted_iota(jnp.int32, (1, events), 1) < count_in[0, 0, 0]
    spread = jnp.broadcast_to(jnp.where(alive, weight_v[...], 0.0), (events, events))
    diagonal = lax.broadcasted_iota(jnp.int32, (events, events), 0) == lax.broadcasted_iota(
        jnp.int32, (events, events), 1
    )
    column_weight = jnp.sum(jnp.where(diagonal, spread, 0.0), axis=1, keepdims=True)
    col[z, pl.ds(ROWS, events), :] = jnp.broadcast_to(column_weight, (events, LANES))

    lane_row = lax.broadcasted_iota(jnp.int32, (LANES, template), 0)
    domains = [lax.rem(z + d, nz) for d in range(nz)]

    def lane_factor(domain):
        member_lane = atoms[domain] & (LANES - 1)
        for e in range(events):
            hot = jnp.where(member_lane[e : e + 1] == lane_row, 1.0, 0.0)
            lanes_hot[domain, :, pl.ds(e * template, template)] = hot.astype(jnp.bfloat16)

    pl.semaphore_wait(barrier, len(greeted))

    column_copies = []
    for d in range(1, nz):
        for part, ref in enumerate((col, atoms)):
            copy = pltpu.make_async_remote_copy(
                src_ref=ref.at[z],
                dst_ref=ref.at[z],
                send_sem=col_sem.at[0, part, d - 1],
                recv_sem=col_sem.at[1, part, d - 1],
                device_id=peer(0, 0, d),
                device_id_type=MESH,
            )
            copy.start()
            column_copies.append(copy)

    def send_around(ref, rows, which):
        for a, b, c in around:
            j = (a * 3 + b) * 3 + c
            pltpu.make_async_remote_copy(
                src_ref=ref.at[pl.ds(home * ROWS, rows)],
                dst_ref=ref.at[pl.ds(j * ROWS, rows)],
                send_sem=send_sem.at[which],
                recv_sem=recv_sem.at[which],
                device_id=peer(1 - a, 1 - b, 1 - c),
                device_id_type=MESH,
            ).start()

    def wait_total(ref, rows, sem):
        part = ref.at[pl.ds(0, rows)]
        pltpu.make_async_copy(part, part, sem).wait()

    send_around(speeds, ROWS, 0)
    for load in loads[5:]:
        load.wait()

    lane_factor(z)
    for copy in column_copies:
        copy.wait_recv()
    for d in range(1, nz):
        lane_factor(lax.rem(z - d + nz, nz))

    members = jnp.concatenate([atoms[domain] for domain in domains], axis=0)
    weights = jnp.concatenate([col[domain, pl.ds(ROWS, events), :] for domain in domains], axis=0)
    total_events = nz * events
    member_chunk = lax.shift_right_logical(members, 7)
    member_lane = members & (LANES - 1)
    centred = []
    for i in range(3):
        taken = jnp.zeros((total_events, template), jnp.float32)
        for d in range(nz):
            for chunk in range(chunks):
                source = jnp.broadcast_to(
                    col[d, pl.ds(i * chunks + chunk, 1), :], (total_events, LANES)
                )
                picked = lane_gather(source, member_lane)
                taken = jnp.where(member_chunk == d * chunks + chunk, picked, taken)
        mean = jnp.sum(taken, axis=1, keepdims=True) * (1.0 / template)
        centred.append(taken - mean)
    shifted = jnp.dot(
        jnp.concatenate(centred, axis=0),
        tmap[...],
        precision=lax.Precision.HIGHEST,
        preferred_element_type=jnp.float32,
    )
    for i in range(3):
        shift = shifted[i * total_events : (i + 1) * total_events] * weights
        coarse = shift.astype(jnp.bfloat16).astype(jnp.float32)
        shifts[i] = coarse
        shifts[3 + i] = shift - coarse

    column_chunks = nz * chunks
    chunk_row = lax.broadcasted_iota(jnp.int32, (column_chunks, template), 0)
    summed = jnp.zeros((6 * column_chunks, LANES), jnp.float32)
    for d, domain in enumerate(domains):
        for first in range(0, events, 2):
            left = []
            for e in range(d * events + first, d * events + first + 2):
                here = member_chunk[e : e + 1] == chunk_row
                parts = [jnp.where(here, shifts[q, pl.ds(e, 1), :], 0.0) for q in range(6)]
                left.append(jnp.concatenate(parts, axis=0))
            summed = summed + lax.dot_general(
                jnp.concatenate(left, axis=1).astype(jnp.bfloat16),
                lanes_hot[domain, :, pl.ds(first * template, 2 * template)],
                (((1,), (1,)), ((), ())),
                preferred_element_type=jnp.float32,
            )
    half = 3 * column_chunks
    displaced = summed[:half] + summed[half:]
    for d in range(nz):
        pieces = [
            displaced[i * column_chunks + d * chunks : i * column_chunks + (d + 1) * chunks]
            for i in range(3)
        ]
        pieces.append(jnp.zeros((chunks, LANES), jnp.float32))
        moved[d] = col[d, pl.ds(0, ROWS), :] + jnp.concatenate(pieces, axis=0)

    def place_of(slot):
        return pl.ds(slot * ROWS, COORDS)

    for c in range(3):
        table[place_of(home - 1 + c), :] = moved[lax.rem(z + c - 1 + nz, nz), pl.ds(0, COORDS), :]
    for a, b in beside:
        for c in depth_offsets:
            pltpu.make_async_remote_copy(
                src_ref=table.at[place_of(home - 1 + c)],
                dst_ref=table.at[place_of((a * 3 + b) * 3 + c)],
                send_sem=send_sem.at[1],
                recv_sem=recv_sem.at[1],
                device_id=peer(1 - a, 1 - b, 0),
                device_id_type=MESH,
            ).start()
    wait_total(speeds, len(around) * ROWS, recv_sem.at[0])
    for a, b, c in around + [(1, 1, 1)]:
        j = (a * 3 + b) * 3 + c
        for s in copies(j)[1:]:
            strengths = pl.ds(s * ROWS + COORDS, ROWS - COORDS)
            speeds[strengths, :] = speeds[pl.ds(j * ROWS + COORDS, ROWS - COORDS), :]

    def pick(source, index):
        lane, part = index & (LANES - 1), lax.shift_right_logical(index, 7)
        picked = lane_gather(source[0], lane)
        for t in range(1, chunks):
            picked = jnp.where(part == t, lane_gather(source[t], lane), picked)
        return picked

    for group in range(slots // 8):
        rows = pl.ds(group * 8, 8)
        source = [
            speeds[pl.ds(group * 8 * ROWS + COORDS + t, 8, stride=ROWS), :] for t in range(chunks)
        ]
        for chunk in range(chunks):
            lanes = pl.ds(chunk * LANES, LANES)
            own = speeds[pl.ds(home * ROWS + COORDS + chunk, 1), :]
            factor[rows, lanes] = (
                own
                * pick(source, nbr[rows, lanes])
                * live[rows, lanes].astype(jnp.float32)
                * (1.0 / (width_scale * width_scale))
            )

    wait_total(table, len(beside) * depths * COORDS, recv_sem.at[1])
    for a, b in beside:
        for c in depth_offsets:
            j = (a * 3 + b) * 3 + c
            for s in copies(j)[1:]:
                table[place_of(s), :] = table[place_of(j), :]
    for c in range(3):
        j = home - 1 + c
        for s in range(j + 27, slots, 27):
            table[place_of(s), :] = table[place_of(j), :]

    def pair_forces(where, result):
        total = [[jnp.zeros((8, LANES), jnp.float32)] * 3 for _ in range(chunks)]
        for group in range(slots // 8):
            source = [
                [
                    where[pl.ds(group * 8 * ROWS + i * chunks + t, 8, stride=ROWS), :]
                    for t in range(chunks)
                ]
                for i in range(3)
            ]
            for chunk in range(chunks):
                rows, lanes = pl.ds(group * 8, 8), pl.ds(chunk * LANES, LANES)
                index = nbr[rows, lanes]
                apart = [
                    where[pl.ds(home * ROWS + i * chunks + chunk, 1), :] - pick(source[i], index)
                    for i in range(3)
                ]
                square = apart[0] * apart[0] + apart[1] * apart[1] + apart[2] * apart[2]
                strength = factor[rows, lanes] * jnp.exp(
                    square * (-0.5 / (width_scale * width_scale))
                )
                total[chunk] = [total[chunk][i] + strength * apart[i] for i in range(3)]
        for chunk in range(chunks):
            for i in range(3):
                result[pl.ds(home * ROWS + i * chunks + chunk, 1), :] = jnp.sum(
                    total[chunk][i], axis=0, keepdims=True
                )

    most = max(len(stage) for stage in stages) + 1

    def fold(value):
        return jnp.sum(value, axis=0, keepdims=True)

    lane_index = lax.broadcasted_iota(jnp.int32, (1, LANES), 1)

    def sum_row(force, speed):
        parts = [fold(force * speed), fold(speed * speed), fold(force * force)]
        power, speed_sq, force_sq = [jnp.sum(part, axis=1, keepdims=True) for part in parts]
        row = jnp.where(lane_index == 0, power, jnp.where(lane_index == 1, speed_sq, 0.0))
        return jnp.where(lane_index == 2, force_sq, row)

    def stage_start(row, which, s):
        base = (which * len(stages) + s) * most
        sums[base] = row
        for slot, offset in enumerate((alone, stages)[which][s]):
            pltpu.make_async_remote_copy(
                src_ref=sums.at[base],
                dst_ref=sums.at[base + 1 + slot],
                send_sem=sum_send.at[which, s],
                recv_sem=sum_recv.at[which, s],
                device_id=peer(*offset),
                device_id_type=MESH,
            ).start()

    def sum_finish(which):
        for s, stage in enumerate((alone, stages)[which]):
            base = (which * len(stages) + s) * most
            if stage:
                wait_total(sums, len(stage), sum_recv.at[which, s])
            row = jnp.sum(sums[pl.ds(base, len(stage) + 1)], axis=0)
            if s + 1 < len(stages):
                stage_start(row, which, s + 1)
        if which == 0:
            wait_total(forces, len(around) * (COORDS + 1), recv_sem.at[2])
            if direct:
                for a, b, c in around:
                    j = (a * 3 + b) * 3 + c
                    row = row + forces[pl.ds(j * ROWS + COORDS, 1), :]
        power, speed_sq, force_sq = row[:, 0:1], row[:, 1:2], row[:, 2:3]
        cosine = power / (jnp.sqrt(speed_sq + epsilon) * jnp.sqrt(force_sq + epsilon))
        ratio = jnp.sqrt((speed_sq + epsilon) / (force_sq + epsilon))
        keep = 0.5 * (1.0 + cosine)
        return keep * (1.0 - mixing), keep * mixing * ratio + time_step

    def block(ref, j):
        return ref[pl.ds(j * ROWS, COORDS), :]

    pair_forces(table, forces)
    row = sum_row(block(forces, home), block(speeds, home))
    forces[pl.ds(home * ROWS + COORDS, 1), :] = row
    send_around(forces, COORDS + 1, 2)
    stage_start(row, 0, 0)
    old, new = sum_finish(0)
    for a, b, c in around + [(1, 1, 1)]:
        j = (a * 3 + b) * 3 + c
        later = table[place_of(j), :] + time_step * (
            old * block(speeds, j) + new * block(forces, j)
        )
        for s in copies(j):
            table2[place_of(s), :] = later
    speed = old * block(speeds, home) + new * block(forces, home)

    pair_forces(table2, forces2)
    force = block(forces2, home)
    stage_start(sum_row(force, speed), 1, 0)
    old, new = sum_finish(1)
    speed = old * speed + new * force
    place = table2[place_of(home), :] + time_step * speed
    for chunk in range(chunks):
        lanes = pl.ds(chunk * LANES, LANES)
        for i in range(3):
            row = i * chunks + chunk
            pos_out[i, :, lanes] = place[row : row + 1]
            vel_out[i, :, lanes] = speed[row : row + 1]
    for copy in column_copies:
        copy.wait_send()
    wait_total(speeds, len(around) * ROWS, send_sem.at[0])
    wait_total(table, len(beside) * depths * COORDS, send_sem.at[1])
    wait_total(forces, len(around) * (COORDS + 1), send_sem.at[2])
    for which in range(2):
        for s, stage in enumerate((alone, stages)[which]):
            if stage:
                wait_total(sums, len(stage), sum_send.at[which, s])


def shards(
    mesh_shape,
    positions,
    velocity,
    atom_eps,
    neighbours,
    pair_live,
    event_count,
    event_atoms,
    event_weight,
    template_map,
):
    atom_count = positions.shape[4]
    slots = neighbours.shape[3]
    events, template = event_atoms.shape[3:]
    nz = mesh_shape[2]
    stages = len(sum_stages(mesh_shape))
    most = max(len(stage) for stage in sum_stages(mesh_shape)) + 1
    f32, i32 = jnp.float32, jnp.int32
    blocks = pltpu.VMEM((slots * ROWS, LANES), f32)
    outs = pl.pallas_call(
        functools.partial(cycle_kernel, mesh_shape),
        out_shape=[jax.ShapeDtypeStruct((3, 1, atom_count), f32)] * 2,
        in_specs=[pl.BlockSpec(memory_space=pltpu.HBM)] * 5
        + [pl.BlockSpec(memory_space=pltpu.SMEM)]
        + [pl.BlockSpec(memory_space=pltpu.HBM)] * 3,
        out_specs=[pl.BlockSpec(memory_space=pltpu.VMEM)] * 2,
        scratch_shapes=[
            pltpu.VMEM((3, 1, atom_count), f32),
            pltpu.VMEM((3, 1, atom_count), f32),
            pltpu.VMEM((1, atom_count), f32),
            pltpu.VMEM((slots, atom_count), i32),
            pltpu.VMEM((slots, atom_count), i32),
            pltpu.VMEM((nz, events, template), i32),
            pltpu.VMEM((1, events), f32),
            pltpu.VMEM((template, template), f32),
            pltpu.VMEM((nz, ROWS + events, LANES), f32),
            pltpu.VMEM((nz, ROWS, LANES), f32),
            pltpu.VMEM((6, nz * events, template), f32),
            pltpu.VMEM((nz, LANES, events * template), jnp.bfloat16),
            pltpu.VMEM((slots, atom_count), f32),
            blocks,
            blocks,
            blocks,
            blocks,
            blocks,
            pltpu.VMEM((2 * stages * most, 1, LANES), f32),
            pltpu.SemaphoreType.DMA((8,)),
            pltpu.SemaphoreType.DMA((2, 2, nz - 1)),
            pltpu.SemaphoreType.DMA((3,)),
            pltpu.SemaphoreType.DMA((3,)),
            pltpu.SemaphoreType.DMA((2, stages)),
            pltpu.SemaphoreType.DMA((2, stages)),
        ],
        compiler_params=pltpu.CompilerParams(
            collective_id=0, has_side_effects=True, vmem_limit_bytes=56520704
        ),
        cost_estimate=pl.CostEstimate(flops=10**7, bytes_accessed=10**6, transcendentals=10**5),
    )(
        positions.reshape(3, 1, atom_count),
        velocity.reshape(3, 1, atom_count),
        atom_eps.reshape(1, atom_count),
        neighbours.reshape(slots, atom_count),
        pair_live.reshape(slots, atom_count),
        event_count,
        event_atoms.reshape(events, template),
        event_weight.reshape(1, events),
        template_map,
    )
    return tuple(result.reshape(positions.shape) for result in outs)


def solution(mesh):
    in_specs = (
        P(None, "gx", "gy", "gz", None),
        P(None, "gx", "gy", "gz", None),
        P("gx", "gy", "gz", None),
        P("gx", "gy", "gz", None, None),
        P("gx", "gy", "gz", None, None),
        P("gx", "gy", "gz"),
        P("gx", "gy", "gz", None, None),
        P("gx", "gy", "gz", None),
        P(),
    )
    out_specs = (P(None, "gx", "gy", "gz", None), P(None, "gx", "gy", "gz", None))
    mesh_shape = tuple(mesh.shape[axis] for axis in ("gx", "gy", "gz"))
    return jax.shard_map(
        functools.partial(shards, mesh_shape),
        mesh=mesh,
        in_specs=in_specs,
        out_specs=out_specs,
        check_vma=False,
    )
```

```python
import functools

import jax
import jax.numpy as jnp
from jax import lax
from jax.experimental import pallas as pl
from jax.experimental.pallas import tpu as pltpu
from jax.sharding import PartitionSpec as P

width_scale = 1.5
time_step = 0.1
mixing = 0.1
epsilon = 1e-06

MESH = pl.DeviceIdType.MESH
LANES = 128
COORDS = 12
ROWS = 16
DIRECT = 64


def lane_gather(table, index):
    return jnp.take_along_axis(table, index, axis=1, mode="promise_in_bounds")


def sum_stages(mesh_shape):
    nx, ny, nz = mesh_shape
    if nx >= 3 and ny >= 3 and nx * ny * nz <= DIRECT:
        every = [(dx, dy, dz) for dx in range(nx) for dy in range(ny) for dz in range(nz)]
        return [sorted(every[1:], key=lambda offset: -sum(map(bool, offset)))]
    return [
        [(d, 0, 0) for d in range(1, nx)],
        [(0, 0, d) for d in range(1, nz)],
        [(0, d, 0) for d in range(1, ny)],
    ]


def cycle_kernel(
    mesh_shape,
    pos_in,
    vel_in,
    eps_in,
    nbr_in,
    live_in,
    count_in,
    atoms_in,
    weight_in,
    map_in,
    pos_out,
    vel_out,
    pos_v,
    vel_v,
    eps_v,
    nbr,
    live,
    atoms,
    weight_v,
    tmap,
    col,
    moved,
    shifts,
    lanes_hot,
    factor,
    table,
    table2,
    speeds,
    forces,
    forces2,
    sums,
    local_sem,
    col_sem,
    send_sem,
    recv_sem,
    sum_send,
    sum_recv,
):
    nx, ny, nz = mesh_shape
    x, y, z = lax.axis_index("gx"), lax.axis_index("gy"), lax.axis_index("gz")
    slots, atom_count = nbr.shape
    events, template = atoms.shape[1:]
    chunks = atom_count // LANES
    home = 13
    depth_offsets = (0, 1) if nz == 2 else (0, 1, 2)
    depths = len(depth_offsets)

    def peer(dx, dy, dz):
        return (
            lax.rem(x + dx + nx, nx),
            lax.rem(y + dy + ny, ny),
            lax.rem(z + dz + nz, nz),
        )

    def copies(j):
        dirs = [j] if nz > 2 or j % 3 != 0 else [j, j + 2]
        return [s for d in dirs for s in range(d, slots, 27)]

    around = [
        (a, b, c)
        for a in range(3)
        for b in range(3)
        for c in depth_offsets
        if (a, b, c) != (1, 1, 1)
    ]
    around.sort(key=lambda direction: -sum(d != 1 for d in direction))
    beside = [(a, b) for a in range(3) for b in range(3) if (a, b) != (1, 1)]
    beside.sort(key=lambda direction: -sum(d != 1 for d in direction))
    stages = sum_stages(mesh_shape)
    direct = len(stages) == 1
    near = {((1 - a) % nx, (1 - b) % ny, (1 - c) % nz) for a, b, c in around}
    alone = [[offset for offset in stages[0] if offset not in near]] if direct else stages
    greeted = {((1 - a) % nx, (1 - b) % ny, (1 - c) % nz) for a, b, c in around}
    greeted |= {((a - 1) % nx, (b - 1) % ny, (c - 1) % nz) for a, b, c in around}
    greeted |= {offset for stage in stages for offset in stage}
    greeted |= {(0, 0, d) for d in range(1, nz)}
    greeted = sorted(greeted)

    barrier = pltpu.get_barrier_semaphore()
    for offset in greeted:
        pl.semaphore_signal(barrier, inc=1, device_id=peer(*offset), device_id_type=MESH)

    own_atoms = atoms.at[z]
    pairs = [
        (pos_in, pos_v),
        (vel_in, vel_v),
        (eps_in, eps_v),
        (weight_in, weight_v),
        (atoms_in, own_atoms),
        (map_in, tmap),
        (nbr_in, nbr),
        (live_in, live),
    ]
    loads = [
        pltpu.make_async_copy(src, dst, local_sem.at[i]) for i, (src, dst) in enumerate(pairs)
    ]
    for load in loads:
        load.start()
    for load in loads[:5]:
        load.wait()

    for chunk in range(chunks):
        lanes = pl.ds(chunk * LANES, LANES)
        for i in range(3):
            row = i * chunks + chunk
            col[z, pl.ds(row, 1), :] = pos_v[i, :, lanes]
            speeds[pl.ds(home * ROWS + row, 1), :] = vel_v[i, :, lanes]
        row = 3 * chunks + chunk
        col[z, pl.ds(row, 1), :] = jnp.sqrt(eps_v[:, lanes])
        speeds[pl.ds(home * ROWS + row, 1), :] = col[z, pl.ds(row, 1), :]
    alive = lax.broadcasted_iota(jnp.int32, (1, events), 1) < count_in[0, 0, 0]
    spread = jnp.broadcast_to(jnp.where(alive, weight_v[...], 0.0), (events, events))
    diagonal = lax.broadcasted_iota(jnp.int32, (events, events), 0) == lax.broadcasted_iota(
        jnp.int32, (events, events), 1
    )
    column_weight = jnp.sum(jnp.where(diagonal, spread, 0.0), axis=1, keepdims=True)
    col[z, pl.ds(ROWS, events), :] = jnp.broadcast_to(column_weight, (events, LANES))

    lane_row = lax.broadcasted_iota(jnp.int32, (LANES, template), 0)
    domains = [lax.rem(z + d, nz) for d in range(nz)]

    def lane_factor(domain):
        member_lane = atoms[domain] & (LANES - 1)
        for e in range(events):
            hot = jnp.where(member_lane[e : e + 1] == lane_row, 1.0, 0.0)
            lanes_hot[domain, :, pl.ds(e * template, template)] = hot.astype(jnp.bfloat16)

    pl.semaphore_wait(barrier, len(greeted))

    column_copies = []
    for d in range(1, nz):
        for part, ref in enumerate((col, atoms)):
            copy = pltpu.make_async_remote_copy(
                src_ref=ref.at[z],
                dst_ref=ref.at[z],
                send_sem=col_sem.at[0, part, d - 1],
                recv_sem=col_sem.at[1, part, d - 1],
                device_id=peer(0, 0, d),
                device_id_type=MESH,
            )
            copy.start()
            column_copies.append(copy)

    def send_around(ref, rows, which):
        for a, b, c in around:
            j = (a * 3 + b) * 3 + c
            pltpu.make_async_remote_copy(
                src_ref=ref.at[pl.ds(home * ROWS, rows)],
                dst_ref=ref.at[pl.ds(j * ROWS, rows)],
                send_sem=send_sem.at[which],
                recv_sem=recv_sem.at[which],
                device_id=peer(1 - a, 1 - b, 1 - c),
                device_id_type=MESH,
            ).start()

    def wait_total(ref, rows, sem):
        part = ref.at[pl.ds(0, rows)]
        pltpu.make_async_copy(part, part, sem).wait()

    send_around(speeds, ROWS, 0)
    for load in loads[5:]:
        load.wait()

    lane_factor(z)
    for copy in column_copies:
        copy.wait_recv()
    for d in range(1, nz):
        lane_factor(lax.rem(z - d + nz, nz))

    members = jnp.concatenate([atoms[domain] for domain in domains], axis=0)
    weights = jnp.concatenate([col[domain, pl.ds(ROWS, events), :] for domain in domains], axis=0)
    total_events = nz * events
    member_chunk = lax.shift_right_logical(members, 7)
    member_lane = members & (LANES - 1)
    centred = []
    for i in range(3):
        taken = jnp.zeros((total_events, template), jnp.float32)
        for d in range(nz):
            for chunk in range(chunks):
                source = jnp.broadcast_to(
                    col[d, pl.ds(i * chunks + chunk, 1), :], (total_events, LANES)
                )
                picked = lane_gather(source, member_lane)
                taken = jnp.where(member_chunk == d * chunks + chunk, picked, taken)
        mean = jnp.sum(taken, axis=1, keepdims=True) * (1.0 / template)
        centred.append(taken - mean)
    shifted = jnp.dot(
        jnp.concatenate(centred, axis=0),
        tmap[...],
        precision=lax.Precision.HIGHEST,
        preferred_element_type=jnp.float32,
    )
    for i in range(3):
        shift = shifted[i * total_events : (i + 1) * total_events] * weights
        coarse = shift.astype(jnp.bfloat16).astype(jnp.float32)
        shifts[i] = coarse
        shifts[3 + i] = shift - coarse

    column_chunks = nz * chunks
    chunk_row = lax.broadcasted_iota(jnp.int32, (column_chunks, template), 0)
    summed = jnp.zeros((6 * column_chunks, LANES), jnp.float32)
    for d, domain in enumerate(domains):
        for first in range(0, events, 2):
            left = []
            for e in range(d * events + first, d * events + first + 2):
                here = member_chunk[e : e + 1] == chunk_row
                parts = [jnp.where(here, shifts[q, pl.ds(e, 1), :], 0.0) for q in range(6)]
                left.append(jnp.concatenate(parts, axis=0))
            summed = summed + lax.dot_general(
                jnp.concatenate(left, axis=1).astype(jnp.bfloat16),
                lanes_hot[domain, :, pl.ds(first * template, 2 * template)],
                (((1,), (1,)), ((), ())),
                preferred_element_type=jnp.float32,
            )
    half = 3 * column_chunks
    displaced = summed[:half] + summed[half:]
    for d in range(nz):
        pieces = [
            displaced[i * column_chunks + d * chunks : i * column_chunks + (d + 1) * chunks]
            for i in range(3)
        ]
        pieces.append(jnp.zeros((chunks, LANES), jnp.float32))
        moved[d] = col[d, pl.ds(0, ROWS), :] + jnp.concatenate(pieces, axis=0)

    def place_of(slot):
        return pl.ds(slot * ROWS, COORDS)

    for c in range(3):
        table[place_of(home - 1 + c), :] = moved[lax.rem(z + c - 1 + nz, nz), pl.ds(0, COORDS), :]
    for a, b in beside:
        for c in depth_offsets:
            pltpu.make_async_remote_copy(
                src_ref=table.at[place_of(home - 1 + c)],
                dst_ref=table.at[place_of((a * 3 + b) * 3 + c)],
                send_sem=send_sem.at[1],
                recv_sem=recv_sem.at[1],
                device_id=peer(1 - a, 1 - b, 0),
                device_id_type=MESH,
            ).start()
    wait_total(speeds, len(around) * ROWS, recv_sem.at[0])
    for a, b, c in around + [(1, 1, 1)]:
        j = (a * 3 + b) * 3 + c
        for s in copies(j)[1:]:
            strengths = pl.ds(s * ROWS + COORDS, ROWS - COORDS)
            speeds[strengths, :] = speeds[pl.ds(j * ROWS + COORDS, ROWS - COORDS), :]

    def pick(source, index):
        lane, part = index & (LANES - 1), lax.shift_right_logical(index, 7)
        picked = lane_gather(source[0], lane)
        for t in range(1, chunks):
            picked = jnp.where(part == t, lane_gather(source[t], lane), picked)
        return picked

    for group in range(slots // 8):
        rows = pl.ds(group * 8, 8)
        source = [
            speeds[pl.ds(group * 8 * ROWS + COORDS + t, 8, stride=ROWS), :] for t in range(chunks)
        ]
        for chunk in range(chunks):
            lanes = pl.ds(chunk * LANES, LANES)
            own = speeds[pl.ds(home * ROWS + COORDS + chunk, 1), :]
            factor[rows, lanes] = (
                own
                * pick(source, nbr[rows, lanes])
                * live[rows, lanes].astype(jnp.float32)
                * (1.0 / (width_scale * width_scale))
            )

    wait_total(table, len(beside) * depths * COORDS, recv_sem.at[1])
    for a, b in beside:
        for c in depth_offsets:
            j = (a * 3 + b) * 3 + c
            for s in copies(j)[1:]:
                table[place_of(s), :] = table[place_of(j), :]
    for c in range(3):
        j = home - 1 + c
        for s in range(j + 27, slots, 27):
            table[place_of(s), :] = table[place_of(j), :]

    def pair_forces(where, result):
        total = [[jnp.zeros((8, LANES), jnp.float32)] * 3 for _ in range(chunks)]
        for group in range(slots // 8):
            source = [
                [
                    where[pl.ds(group * 8 * ROWS + i * chunks + t, 8, stride=ROWS), :]
                    for t in range(chunks)
                ]
                for i in range(3)
            ]
            for chunk in range(chunks):
                rows, lanes = pl.ds(group * 8, 8), pl.ds(chunk * LANES, LANES)
                index = nbr[rows, lanes]
                apart = [
                    where[pl.ds(home * ROWS + i * chunks + chunk, 1), :] - pick(source[i], index)
                    for i in range(3)
                ]
                square = apart[0] * apart[0] + apart[1] * apart[1] + apart[2] * apart[2]
                strength = factor[rows, lanes] * jnp.exp(
                    square * (-0.5 / (width_scale * width_scale))
                )
                total[chunk] = [total[chunk][i] + strength * apart[i] for i in range(3)]
        for chunk in range(chunks):
            for i in range(3):
                result[pl.ds(home * ROWS + i * chunks + chunk, 1), :] = jnp.sum(
                    total[chunk][i], axis=0, keepdims=True
                )

    most = max(len(stage) for stage in stages) + 1

    def fold(value):
        return jnp.sum(value, axis=0, keepdims=True)

    lane_index = lax.broadcasted_iota(jnp.int32, (1, LANES), 1)

    def sum_row(force, speed):
        parts = [fold(force * speed), fold(speed * speed), fold(force * force)]
        power, speed_sq, force_sq = [jnp.sum(part, axis=1, keepdims=True) for part in parts]
        row = jnp.where(lane_index == 0, power, jnp.where(lane_index == 1, speed_sq, 0.0))
        return jnp.where(lane_index == 2, force_sq, row)

    def stage_start(row, which, s):
        base = (which * len(stages) + s) * most
        sums[base] = row
        for slot, offset in enumerate((alone, stages)[which][s]):
            pltpu.make_async_remote_copy(
                src_ref=sums.at[base],
                dst_ref=sums.at[base + 1 + slot],
                send_sem=sum_send.at[which, s],
                recv_sem=sum_recv.at[which, s],
                device_id=peer(*offset),
                device_id_type=MESH,
            ).start()

    def sum_finish(which):
        for s, stage in enumerate((alone, stages)[which]):
            base = (which * len(stages) + s) * most
            if stage:
                wait_total(sums, len(stage), sum_recv.at[which, s])
            row = jnp.sum(sums[pl.ds(base, len(stage) + 1)], axis=0)
            if s + 1 < len(stages):
                stage_start(row, which, s + 1)
        if which == 0:
            wait_total(forces, len(around) * (COORDS + 1), recv_sem.at[2])
            if direct:
                for a, b, c in around:
                    j = (a * 3 + b) * 3 + c
                    row = row + forces[pl.ds(j * ROWS + COORDS, 1), :]
        power, speed_sq, force_sq = row[:, 0:1], row[:, 1:2], row[:, 2:3]
        cosine = power / (jnp.sqrt(speed_sq + epsilon) * jnp.sqrt(force_sq + epsilon))
        ratio = jnp.sqrt((speed_sq + epsilon) / (force_sq + epsilon))
        keep = 0.5 * (1.0 + cosine)
        return keep * (1.0 - mixing), keep * mixing * ratio + time_step

    def block(ref, j):
        return ref[pl.ds(j * ROWS, COORDS), :]

    pair_forces(table, forces)
    row = sum_row(block(forces, home), block(speeds, home))
    forces[pl.ds(home * ROWS + COORDS, 1), :] = row
    send_around(forces, COORDS + 1, 2)
    stage_start(row, 0, 0)
    old, new = sum_finish(0)
    for a, b, c in around + [(1, 1, 1)]:
        j = (a * 3 + b) * 3 + c
        later = table[place_of(j), :] + time_step * (
            old * block(speeds, j) + new * block(forces, j)
        )
        for s in copies(j):
            table2[place_of(s), :] = later
    speed = old * block(speeds, home) + new * block(forces, home)

    pair_forces(table2, forces2)
    force = block(forces2, home)
    stage_start(sum_row(force, speed), 1, 0)
    old, new = sum_finish(1)
    speed = old * speed + new * force
    place = table2[place_of(home), :] + time_step * speed
    for chunk in range(chunks):
        lanes = pl.ds(chunk * LANES, LANES)
        for i in range(3):
            row = i * chunks + chunk
            pos_out[i, :, lanes] = place[row : row + 1]
            vel_out[i, :, lanes] = speed[row : row + 1]
    for copy in column_copies:
        copy.wait_send()
    wait_total(speeds, len(around) * ROWS, send_sem.at[0])
    wait_total(table, len(beside) * depths * COORDS, send_sem.at[1])
    wait_total(forces, len(around) * (COORDS + 1), send_sem.at[2])
    for which in range(2):
        for s, stage in enumerate((alone, stages)[which]):
            if stage:
                wait_total(sums, len(stage), sum_send.at[which, s])


def hand_over(pos, vel, pos_out, vel_out, sem):
    both = [
        pltpu.make_async_copy(src, dst, sem.at[i])
        for i, (src, dst) in enumerate(((pos, pos_out), (vel, vel_out)))
    ]
    for copy in both:
        copy.start()
    for copy in both:
        copy.wait()


def shards(
    mesh_shape,
    positions,
    velocity,
    atom_eps,
    neighbours,
    pair_live,
    event_count,
    event_atoms,
    event_weight,
    template_map,
):
    atom_count = positions.shape[4]
    slots = neighbours.shape[3]
    events, template = event_atoms.shape[3:]
    nz = mesh_shape[2]
    stages = len(sum_stages(mesh_shape))
    most = max(len(stage) for stage in sum_stages(mesh_shape)) + 1
    f32, i32 = jnp.float32, jnp.int32
    blocks = pltpu.VMEM((slots * ROWS, LANES), f32)
    outs = pl.pallas_call(
        functools.partial(cycle_kernel, mesh_shape),
        out_shape=[jax.ShapeDtypeStruct((3, 1, atom_count), f32)] * 2,
        in_specs=[pl.BlockSpec(memory_space=pltpu.HBM)] * 5
        + [pl.BlockSpec(memory_space=pltpu.SMEM)]
        + [pl.BlockSpec(memory_space=pltpu.HBM)] * 3,
        out_specs=[pl.BlockSpec(memory_space=pltpu.VMEM)] * 2,
        scratch_shapes=[
            pltpu.VMEM((3, 1, atom_count), f32),
            pltpu.VMEM((3, 1, atom_count), f32),
            pltpu.VMEM((1, atom_count), f32),
            pltpu.VMEM((slots, atom_count), i32),
            pltpu.VMEM((slots, atom_count), i32),
            pltpu.VMEM((nz, events, template), i32),
            pltpu.VMEM((1, events), f32),
            pltpu.VMEM((template, template), f32),
            pltpu.VMEM((nz, ROWS + events, LANES), f32),
            pltpu.VMEM((nz, ROWS, LANES), f32),
            pltpu.VMEM((6, nz * events, template), f32),
            pltpu.VMEM((nz, LANES, events * template), jnp.bfloat16),
            pltpu.VMEM((slots, atom_count), f32),
            blocks,
            blocks,
            blocks,
            blocks,
            blocks,
            pltpu.VMEM((2 * stages * most, 1, LANES), f32),
            pltpu.SemaphoreType.DMA((8,)),
            pltpu.SemaphoreType.DMA((2, 2, nz - 1)),
            pltpu.SemaphoreType.DMA((3,)),
            pltpu.SemaphoreType.DMA((3,)),
            pltpu.SemaphoreType.DMA((2, stages)),
            pltpu.SemaphoreType.DMA((2, stages)),
        ],
        compiler_params=pltpu.CompilerParams(
            collective_id=0, has_side_effects=True, vmem_limit_bytes=56520704
        ),
        cost_estimate=pl.CostEstimate(flops=10**7, bytes_accessed=10**6, transcendentals=10**5),
    )(
        positions.reshape(3, 1, atom_count),
        velocity.reshape(3, 1, atom_count),
        atom_eps.reshape(1, atom_count),
        neighbours.reshape(slots, atom_count),
        pair_live.reshape(slots, atom_count),
        event_count,
        event_atoms.reshape(events, template),
        event_weight.reshape(1, events),
        template_map,
    )
    results = pl.pallas_call(
        hand_over,
        out_shape=[jax.ShapeDtypeStruct((3, 1, atom_count), f32)] * 2,
        in_specs=[pl.BlockSpec(memory_space=pl.ANY)] * 2,
        out_specs=[pl.BlockSpec(memory_space=pl.ANY)] * 2,
        scratch_shapes=[pltpu.SemaphoreType.DMA((2,))],
    )(*outs)
    return tuple(result.reshape(positions.shape) for result in results)


def solution(mesh):
    in_specs = (
        P(None, "gx", "gy", "gz", None),
        P(None, "gx", "gy", "gz", None),
        P("gx", "gy", "gz", None),
        P("gx", "gy", "gz", None, None),
        P("gx", "gy", "gz", None, None),
        P("gx", "gy", "gz"),
        P("gx", "gy", "gz", None, None),
        P("gx", "gy", "gz", None),
        P(),
    )
    out_specs = (P(None, "gx", "gy", "gz", None), P(None, "gx", "gy", "gz", None))
    mesh_shape = tuple(mesh.shape[axis] for axis in ("gx", "gy", "gz"))
    return jax.shard_map(
        functools.partial(shards, mesh_shape),
        mesh=mesh,
        in_specs=in_specs,
        out_specs=out_specs,
        check_vma=False,
    )
```

```python
import functools

import jax
import jax.numpy as jnp
from jax import lax
from jax.experimental import pallas as pl
from jax.experimental.pallas import tpu as pltpu
from jax.sharding import PartitionSpec as P

width_scale = 1.5
time_step = 0.1
mixing = 0.1
epsilon = 1e-06

MESH = pl.DeviceIdType.MESH
LANES = 128
COORDS = 12
ROWS = 16
DIRECT = 64


def lane_gather(table, index):
    return jnp.take_along_axis(table, index, axis=1, mode="promise_in_bounds")


def sum_stages(mesh_shape):
    nx, ny, nz = mesh_shape
    if nx >= 3 and ny >= 3 and nx * ny * nz <= DIRECT:
        every = [(dx, dy, dz) for dx in range(nx) for dy in range(ny) for dz in range(nz)]
        return [sorted(every[1:], key=lambda offset: -sum(map(bool, offset)))]
    return [
        [(d, 0, 0) for d in range(1, nx)],
        [(0, 0, d) for d in range(1, nz)],
        [(0, d, 0) for d in range(1, ny)],
    ]


def cycle_kernel(
    mesh_shape,
    pos_in,
    vel_in,
    eps_in,
    nbr_in,
    live_in,
    count_in,
    atoms_in,
    weight_in,
    map_in,
    pos_out,
    vel_out,
    pos_v,
    vel_v,
    eps_v,
    nbr,
    live,
    atoms,
    weight_v,
    tmap,
    col,
    moved,
    shifts,
    lanes_hot,
    factor,
    table,
    table2,
    speeds,
    forces,
    forces2,
    sums,
    local_sem,
    col_sem,
    send_sem,
    recv_sem,
    sum_send,
    sum_recv,
):
    nx, ny, nz = mesh_shape
    x, y, z = lax.axis_index("gx"), lax.axis_index("gy"), lax.axis_index("gz")
    slots, atom_count = nbr.shape
    events, template = atoms.shape[1:]
    chunks = atom_count // LANES
    home = 13
    depth_offsets = (0, 1) if nz == 2 else (0, 1, 2)
    depths = len(depth_offsets)

    def peer(dx, dy, dz):
        return (
            lax.rem(x + dx + nx, nx),
            lax.rem(y + dy + ny, ny),
            lax.rem(z + dz + nz, nz),
        )

    def copies(j):
        dirs = [j] if nz > 2 or j % 3 != 0 else [j, j + 2]
        return [s for d in dirs for s in range(d, slots, 27)]

    around = [
        (a, b, c)
        for a in range(3)
        for b in range(3)
        for c in depth_offsets
        if (a, b, c) != (1, 1, 1)
    ]
    around.sort(key=lambda direction: -sum(d != 1 for d in direction))
    beside = [(a, b) for a in range(3) for b in range(3) if (a, b) != (1, 1)]
    beside.sort(key=lambda direction: -sum(d != 1 for d in direction))
    stages = sum_stages(mesh_shape)
    direct = len(stages) == 1
    near = {((1 - a) % nx, (1 - b) % ny, (1 - c) % nz) for a, b, c in around}
    alone = [[offset for offset in stages[0] if offset not in near]] if direct else stages
    greeted = {((1 - a) % nx, (1 - b) % ny, (1 - c) % nz) for a, b, c in around}
    greeted |= {((a - 1) % nx, (b - 1) % ny, (c - 1) % nz) for a, b, c in around}
    greeted |= {offset for stage in stages for offset in stage}
    greeted |= {(0, 0, d) for d in range(1, nz)}
    greeted = sorted(greeted)

    barrier = pltpu.get_barrier_semaphore()
    for offset in greeted:
        pl.semaphore_signal(barrier, inc=1, device_id=peer(*offset), device_id_type=MESH)

    own_atoms = atoms.at[z]
    pairs = [
        (pos_in, pos_v),
        (vel_in, vel_v),
        (eps_in, eps_v),
        (weight_in, weight_v),
        (atoms_in, own_atoms),
        (map_in, tmap),
        (nbr_in, nbr),
        (live_in, live),
    ]
    loads = [
        pltpu.make_async_copy(src, dst, local_sem.at[i]) for i, (src, dst) in enumerate(pairs)
    ]
    for load in loads:
        load.start()
    for load in loads[:5]:
        load.wait()

    for chunk in range(chunks):
        lanes = pl.ds(chunk * LANES, LANES)
        for i in range(3):
            row = i * chunks + chunk
            col[z, pl.ds(row, 1), :] = pos_v[i, :, lanes]
            speeds[pl.ds(home * ROWS + row, 1), :] = vel_v[i, :, lanes]
        row = 3 * chunks + chunk
        col[z, pl.ds(row, 1), :] = jnp.sqrt(eps_v[:, lanes])
        speeds[pl.ds(home * ROWS + row, 1), :] = col[z, pl.ds(row, 1), :]
    alive = lax.broadcasted_iota(jnp.int32, (1, events), 1) < count_in[0, 0, 0]
    spread = jnp.broadcast_to(jnp.where(alive, weight_v[...], 0.0), (events, events))
    diagonal = lax.broadcasted_iota(jnp.int32, (events, events), 0) == lax.broadcasted_iota(
        jnp.int32, (events, events), 1
    )
    column_weight = jnp.sum(jnp.where(diagonal, spread, 0.0), axis=1, keepdims=True)
    col[z, pl.ds(ROWS, events), :] = jnp.broadcast_to(column_weight, (events, LANES))

    lane_row = lax.broadcasted_iota(jnp.int32, (LANES, template), 0)
    domains = [lax.rem(z + d, nz) for d in range(nz)]

    def lane_factor(domain):
        member_lane = atoms[domain] & (LANES - 1)
        for e in range(events):
            hot = jnp.where(member_lane[e : e + 1] == lane_row, 1.0, 0.0)
            lanes_hot[domain, :, pl.ds(e * template, template)] = hot.astype(jnp.bfloat16)

    pl.semaphore_wait(barrier, len(greeted))

    column_copies = []
    for d in range(1, nz):
        for part, ref in enumerate((col, atoms)):
            copy = pltpu.make_async_remote_copy(
                src_ref=ref.at[z],
                dst_ref=ref.at[z],
                send_sem=col_sem.at[0, part, d - 1],
                recv_sem=col_sem.at[1, part, d - 1],
                device_id=peer(0, 0, d),
                device_id_type=MESH,
            )
            copy.start()
            column_copies.append(copy)

    def send_around(ref, rows, which, chosen):
        for a, b, c in chosen:
            j = (a * 3 + b) * 3 + c
            pltpu.make_async_remote_copy(
                src_ref=ref.at[pl.ds(home * ROWS, rows)],
                dst_ref=ref.at[pl.ds(j * ROWS, rows)],
                send_sem=send_sem.at[which],
                recv_sem=recv_sem.at[which],
                device_id=peer(1 - a, 1 - b, 1 - c),
                device_id_type=MESH,
            ).start()

    def wait_total(ref, rows, sem):
        part = ref.at[pl.ds(0, rows)]
        pltpu.make_async_copy(part, part, sem).wait()

    send_around(speeds, ROWS, 0, [way for way in around if way[2] == 1])
    for load in loads[5:]:
        load.wait()

    lane_factor(z)
    for copy in column_copies:
        copy.wait_recv()
    send_around(speeds, ROWS, 0, [way for way in around if way[2] != 1])
    for d in range(1, nz):
        lane_factor(lax.rem(z - d + nz, nz))

    members = jnp.concatenate([atoms[domain] for domain in domains], axis=0)
    weights = jnp.concatenate([col[domain, pl.ds(ROWS, events), :] for domain in domains], axis=0)
    total_events = nz * events
    member_chunk = lax.shift_right_logical(members, 7)
    member_lane = members & (LANES - 1)
    centred = []
    for i in range(3):
        taken = jnp.zeros((total_events, template), jnp.float32)
        for d in range(nz):
            for chunk in range(chunks):
                source = jnp.broadcast_to(
                    col[d, pl.ds(i * chunks + chunk, 1), :], (total_events, LANES)
                )
                picked = lane_gather(source, member_lane)
                taken = jnp.where(member_chunk == d * chunks + chunk, picked, taken)
        mean = jnp.sum(taken, axis=1, keepdims=True) * (1.0 / template)
        centred.append(taken - mean)
    shifted = jnp.dot(
        jnp.concatenate(centred, axis=0),
        tmap[...],
        precision=lax.Precision.HIGHEST,
        preferred_element_type=jnp.float32,
    )
    for i in range(3):
        shift = shifted[i * total_events : (i + 1) * total_events] * weights
        coarse = shift.astype(jnp.bfloat16).astype(jnp.float32)
        shifts[i] = coarse
        shifts[3 + i] = shift - coarse

    column_chunks = nz * chunks
    chunk_row = lax.broadcasted_iota(jnp.int32, (column_chunks, template), 0)
    summed = jnp.zeros((6 * column_chunks, LANES), jnp.float32)
    for d, domain in enumerate(domains):
        for first in range(0, events, 2):
            left = []
            for e in range(d * events + first, d * events + first + 2):
                here = member_chunk[e : e + 1] == chunk_row
                parts = [jnp.where(here, shifts[q, pl.ds(e, 1), :], 0.0) for q in range(6)]
                left.append(jnp.concatenate(parts, axis=0))
            summed = summed + lax.dot_general(
                jnp.concatenate(left, axis=1).astype(jnp.bfloat16),
                lanes_hot[domain, :, pl.ds(first * template, 2 * template)],
                (((1,), (1,)), ((), ())),
                preferred_element_type=jnp.float32,
            )
    half = 3 * column_chunks
    displaced = summed[:half] + summed[half:]
    for d in range(nz):
        pieces = [
            displaced[i * column_chunks + d * chunks : i * column_chunks + (d + 1) * chunks]
            for i in range(3)
        ]
        pieces.append(jnp.zeros((chunks, LANES), jnp.float32))
        moved[d] = col[d, pl.ds(0, ROWS), :] + jnp.concatenate(pieces, axis=0)

    def place_of(slot):
        return pl.ds(slot * ROWS, COORDS)

    for c in range(3):
        table[place_of(home - 1 + c), :] = moved[lax.rem(z + c - 1 + nz, nz), pl.ds(0, COORDS), :]
    for a, b in beside:
        for c in depth_offsets:
            pltpu.make_async_remote_copy(
                src_ref=table.at[place_of(home - 1 + c)],
                dst_ref=table.at[place_of((a * 3 + b) * 3 + c)],
                send_sem=send_sem.at[1],
                recv_sem=recv_sem.at[1],
                device_id=peer(1 - a, 1 - b, 0),
                device_id_type=MESH,
            ).start()
    wait_total(speeds, len(around) * ROWS, recv_sem.at[0])
    for a, b, c in around + [(1, 1, 1)]:
        j = (a * 3 + b) * 3 + c
        for s in copies(j)[1:]:
            strengths = pl.ds(s * ROWS + COORDS, ROWS - COORDS)
            speeds[strengths, :] = speeds[pl.ds(j * ROWS + COORDS, ROWS - COORDS), :]

    def pick(source, index):
        lane, part = index & (LANES - 1), lax.shift_right_logical(index, 7)
        picked = lane_gather(source[0], lane)
        for t in range(1, chunks):
            picked = jnp.where(part == t, lane_gather(source[t], lane), picked)
        return picked

    for group in range(slots // 8):
        rows = pl.ds(group * 8, 8)
        source = [
            speeds[pl.ds(group * 8 * ROWS + COORDS + t, 8, stride=ROWS), :] for t in range(chunks)
        ]
        for chunk in range(chunks):
            lanes = pl.ds(chunk * LANES, LANES)
            own = speeds[pl.ds(home * ROWS + COORDS + chunk, 1), :]
            factor[rows, lanes] = (
                own
                * pick(source, nbr[rows, lanes])
                * live[rows, lanes].astype(jnp.float32)
                * (1.0 / (width_scale * width_scale))
            )

    wait_total(table, len(beside) * depths * COORDS, recv_sem.at[1])
    for a, b in beside:
        for c in depth_offsets:
            j = (a * 3 + b) * 3 + c
            for s in copies(j)[1:]:
                table[place_of(s), :] = table[place_of(j), :]
    for c in range(3):
        j = home - 1 + c
        for s in range(j + 27, slots, 27):
            table[place_of(s), :] = table[place_of(j), :]

    def pair_forces(where, result):
        total = [[jnp.zeros((8, LANES), jnp.float32)] * 3 for _ in range(chunks)]
        for group in range(slots // 8):
            source = [
                [
                    where[pl.ds(group * 8 * ROWS + i * chunks + t, 8, stride=ROWS), :]
                    for t in range(chunks)
                ]
                for i in range(3)
            ]
            for chunk in range(chunks):
                rows, lanes = pl.ds(group * 8, 8), pl.ds(chunk * LANES, LANES)
                index = nbr[rows, lanes]
                apart = [
                    where[pl.ds(home * ROWS + i * chunks + chunk, 1), :] - pick(source[i], index)
                    for i in range(3)
                ]
                square = apart[0] * apart[0] + apart[1] * apart[1] + apart[2] * apart[2]
                strength = factor[rows, lanes] * jnp.exp(
                    square * (-0.5 / (width_scale * width_scale))
                )
                total[chunk] = [total[chunk][i] + strength * apart[i] for i in range(3)]
        for chunk in range(chunks):
            for i in range(3):
                result[pl.ds(home * ROWS + i * chunks + chunk, 1), :] = jnp.sum(
                    total[chunk][i], axis=0, keepdims=True
                )

    most = max(len(stage) for stage in stages) + 1

    def fold(value):
        return jnp.sum(value, axis=0, keepdims=True)

    lane_index = lax.broadcasted_iota(jnp.int32, (1, LANES), 1)

    def sum_row(force, speed):
        parts = [fold(force * speed), fold(speed * speed), fold(force * force)]
        power, speed_sq, force_sq = [jnp.sum(part, axis=1, keepdims=True) for part in parts]
        row = jnp.where(lane_index == 0, power, jnp.where(lane_index == 1, speed_sq, 0.0))
        return jnp.where(lane_index == 2, force_sq, row)

    def stage_start(row, which, s):
        base = (which * len(stages) + s) * most
        sums[base] = row
        for slot, offset in enumerate((alone, stages)[which][s]):
            pltpu.make_async_remote_copy(
                src_ref=sums.at[base],
                dst_ref=sums.at[base + 1 + slot],
                send_sem=sum_send.at[which, s],
                recv_sem=sum_recv.at[which, s],
                device_id=peer(*offset),
                device_id_type=MESH,
            ).start()

    def sum_finish(which):
        for s, stage in enumerate((alone, stages)[which]):
            base = (which * len(stages) + s) * most
            if stage:
                wait_total(sums, len(stage), sum_recv.at[which, s])
            row = jnp.sum(sums[pl.ds(base, len(stage) + 1)], axis=0)
            if s + 1 < len(stages):
                stage_start(row, which, s + 1)
        if which == 0:
            wait_total(forces, len(around) * (COORDS + 1), recv_sem.at[2])
            if direct:
                for a, b, c in around:
                    j = (a * 3 + b) * 3 + c
                    row = row + forces[pl.ds(j * ROWS + COORDS, 1), :]
        power, speed_sq, force_sq = row[:, 0:1], row[:, 1:2], row[:, 2:3]
        cosine = power / (jnp.sqrt(speed_sq + epsilon) * jnp.sqrt(force_sq + epsilon))
        ratio = jnp.sqrt((speed_sq + epsilon) / (force_sq + epsilon))
        keep = 0.5 * (1.0 + cosine)
        return keep * (1.0 - mixing), keep * mixing * ratio + time_step

    def block(ref, j):
        return ref[pl.ds(j * ROWS, COORDS), :]

    pair_forces(table, forces)
    row = sum_row(block(forces, home), block(speeds, home))
    forces[pl.ds(home * ROWS + COORDS, 1), :] = row
    send_around(forces, COORDS + 1, 2, around)
    stage_start(row, 0, 0)
    old, new = sum_finish(0)
    for a, b, c in around + [(1, 1, 1)]:
        j = (a * 3 + b) * 3 + c
        later = table[place_of(j), :] + time_step * (
            old * block(speeds, j) + new * block(forces, j)
        )
        for s in copies(j):
            table2[place_of(s), :] = later
    speed = old * block(speeds, home) + new * block(forces, home)

    pair_forces(table2, forces2)
    force = block(forces2, home)
    stage_start(sum_row(force, speed), 1, 0)
    old, new = sum_finish(1)
    speed = old * speed + new * force
    place = table2[place_of(home), :] + time_step * speed
    for chunk in range(chunks):
        lanes = pl.ds(chunk * LANES, LANES)
        for i in range(3):
            row = i * chunks + chunk
            pos_out[i, :, lanes] = place[row : row + 1]
            vel_out[i, :, lanes] = speed[row : row + 1]
    for copy in column_copies:
        copy.wait_send()
    wait_total(speeds, len(around) * ROWS, send_sem.at[0])
    wait_total(table, len(beside) * depths * COORDS, send_sem.at[1])
    wait_total(forces, len(around) * (COORDS + 1), send_sem.at[2])
    for which in range(2):
        for s, stage in enumerate((alone, stages)[which]):
            if stage:
                wait_total(sums, len(stage), sum_send.at[which, s])


def shards(
    mesh_shape,
    positions,
    velocity,
    atom_eps,
    neighbours,
    pair_live,
    event_count,
    event_atoms,
    event_weight,
    template_map,
):
    atom_count = positions.shape[4]
    slots = neighbours.shape[3]
    events, template = event_atoms.shape[3:]
    nz = mesh_shape[2]
    stages = len(sum_stages(mesh_shape))
    most = max(len(stage) for stage in sum_stages(mesh_shape)) + 1
    f32, i32 = jnp.float32, jnp.int32
    blocks = pltpu.VMEM((slots * ROWS, LANES), f32)
    outs = pl.pallas_call(
        functools.partial(cycle_kernel, mesh_shape),
        out_shape=[jax.ShapeDtypeStruct((3, 1, atom_count), f32)] * 2,
        in_specs=[pl.BlockSpec(memory_space=pltpu.HBM)] * 5
        + [pl.BlockSpec(memory_space=pltpu.SMEM)]
        + [pl.BlockSpec(memory_space=pltpu.HBM)] * 3,
        out_specs=[pl.BlockSpec(memory_space=pltpu.VMEM)] * 2,
        scratch_shapes=[
            pltpu.VMEM((3, 1, atom_count), f32),
            pltpu.VMEM((3, 1, atom_count), f32),
            pltpu.VMEM((1, atom_count), f32),
            pltpu.VMEM((slots, atom_count), i32),
            pltpu.VMEM((slots, atom_count), i32),
            pltpu.VMEM((nz, events, template), i32),
            pltpu.VMEM((1, events), f32),
            pltpu.VMEM((template, template), f32),
            pltpu.VMEM((nz, ROWS + events, LANES), f32),
            pltpu.VMEM((nz, ROWS, LANES), f32),
            pltpu.VMEM((6, nz * events, template), f32),
            pltpu.VMEM((nz, LANES, events * template), jnp.bfloat16),
            pltpu.VMEM((slots, atom_count), f32),
            blocks,
            blocks,
            blocks,
            blocks,
            blocks,
            pltpu.VMEM((2 * stages * most, 1, LANES), f32),
            pltpu.SemaphoreType.DMA((8,)),
            pltpu.SemaphoreType.DMA((2, 2, nz - 1)),
            pltpu.SemaphoreType.DMA((3,)),
            pltpu.SemaphoreType.DMA((3,)),
            pltpu.SemaphoreType.DMA((2, stages)),
            pltpu.SemaphoreType.DMA((2, stages)),
        ],
        compiler_params=pltpu.CompilerParams(
            collective_id=0, has_side_effects=True, vmem_limit_bytes=56520704
        ),
        cost_estimate=pl.CostEstimate(flops=10**7, bytes_accessed=10**6, transcendentals=10**5),
    )(
        positions.reshape(3, 1, atom_count),
        velocity.reshape(3, 1, atom_count),
        atom_eps.reshape(1, atom_count),
        neighbours.reshape(slots, atom_count),
        pair_live.reshape(slots, atom_count),
        event_count,
        event_atoms.reshape(events, template),
        event_weight.reshape(1, events),
        template_map,
    )
    return tuple(result.reshape(positions.shape) for result in outs)


def solution(mesh):
    in_specs = (
        P(None, "gx", "gy", "gz", None),
        P(None, "gx", "gy", "gz", None),
        P("gx", "gy", "gz", None),
        P("gx", "gy", "gz", None, None),
        P("gx", "gy", "gz", None, None),
        P("gx", "gy", "gz"),
        P("gx", "gy", "gz", None, None),
        P("gx", "gy", "gz", None),
        P(),
    )
    out_specs = (P(None, "gx", "gy", "gz", None), P(None, "gx", "gy", "gz", None))
    mesh_shape = tuple(mesh.shape[axis] for axis in ("gx", "gy", "gz"))
    return jax.shard_map(
        functools.partial(shards, mesh_shape),
        mesh=mesh,
        in_specs=in_specs,
        out_specs=out_specs,
        check_vma=False,
    )
```
